32 devices in a mesh: height: 16 (over z, x, core), plan: 2 (over y).
Axes of the slice: x: 2, y: 2, z: 4, core: 2. Of those that a mesh axis runs over, the one named last changes fastest.
Arguments:
- displacement: float32 [3, 16, 40, 256], P(None, 'height', None, 'plan'), may hold values from -3 to 3
- velocity: float32 [3, 16, 40, 256], P(None, 'height', None, 'plan'), may hold values from -3 to 3
- lumped_mass: float32 [16, 40, 256], P('height', None, 'plan'), may hold values from 0.3 to 3
- plastic_strain: float32 [3, 8, 16, 40, 256], P(None, None, 'height', None, 'plan'), may hold values from -1 to 1
- hardening_strain: float32 [3, 8, 16, 40, 256], P(None, None, 'height', None, 'plan'), may hold values from 0.01 to 0.5
- material_ids: int32 [3, 8, 16, 40, 256], P(None, None, 'height', None, 'plan'), may hold values from 0 to 7
- material_table: float32 [8, 3], replicated, may hold values from 0.5 to 2
- ground_accel: float32 [4, 3], replicated, may hold values from -4 to 4
- snapshot_history: bfloat16 [60, 3, 16, 40, 256], P(None, None, 'height', None, 'plan'), may hold values from -6 to 6
- mode_shapes: bfloat16 [256, 3, 16, 40, 256], P(None, None, 'height', None, 'plan'), as said below
Outputs:
- displacement_end: float32 [3, 16, 40, 256], P(None, 'height', None, 'plan')
- velocity_end: float32 [3, 16, 40, 256], P(None, 'height', None, 'plan')
- plastic_end: float32 [3, 8, 16, 40, 256], P(None, None, 'height', None, 'plan')
- hardening_end: float32 [3, 8, 16, 40, 256], P(None, None, 'height', None, 'plan')
- modal_coords: float32 [256, 64], P(('height', 'plan'))
The draws below stay inside these ranges and needn't reach their ends.
Inputs may be any that keep to these rules, and one draw needn't show every extreme that they name: mode_shapes are scaled so that mass_gram is positive definite and well conditioned.
All inputs are finite; a program needn't handle non-finite values.
Results may differ from the reference program's by a relative error of at most 0.0083.
Values sent between devices are 32-bit elements; how exact they have to be, the bound alone decides.
A program may use at most 128 MiB of HBM per device.

```python
import math
import jax
import jax.numpy as jnp
from jax import lax

MODES = 256
SNAP = 64
STEPS = 4
NF = 8
NMAT = 8
QY = 40
HIST = 60
NZ = 16
NP = 256


def draw_mode_shapes(key, part):
    array_shape = (MODES, 3, NZ, QY, NP)
    unit_scale = (3 * NZ * QY * NP) ** (-0.5)
    raw_values = jax.random.normal(key, array_shape, jnp.float32)
    partner = jax.random.permutation(jax.random.fold_in(key, 13), MODES)
    mixed_modes = raw_values + 0.6 * jnp.take(raw_values, partner, axis=0)
    return (mixed_modes * unit_scale).astype(jnp.bfloat16)


def set_ends(array, own_key, low, top_value):
    longest = array.shape.index(max(array.shape))
    spots = []
    for shift in (0, 1):
        where = [jax.random.randint(jax.random.fold_in(own_key, axis), (), 0, length) for axis, length in enumerate(array.shape)]
        where[longest] = (where[longest] + shift) % array.shape[longest]
        spots.append(tuple(where))
    return array.at[spots[0]].set(low).at[spots[1]].set(top_value)


def level_of(rng, extent, shards, least, top_value):
    level = 1.0
    for axis_at, blocks in shards:
        steps = jax.random.uniform(jax.random.fold_in(jax.random.fold_in(rng, 6), axis_at), (blocks,), jnp.float32, least / len(shards), top_value / len(shards))
        level = level * jnp.repeat(jnp.exp(steps), extent[axis_at] // blocks).reshape((-1,) + (1,) * (len(extent) - 1 - axis_at))
    return level


def gaussian(stream_key, dims, spread, most, cuts=(), held_as=jnp.bfloat16):
    entries = jax.random.normal(stream_key, dims, jnp.float32) * spread
    if len(cuts) > 0:
        entries = level_of(stream_key, dims, cuts, -0.22, 0.18) * entries
    return jnp.clip(entries, min=-most, max=most).astype(held_as)


def setup_inputs(seed: int = 0) -> dict:
    arg_keys = jax.random.split(jax.random.key(seed), 11)
    return {
        "displacement": gaussian(arg_keys[0], (3, NZ, QY, NP), 0.5, 3.0, ((1, 16), (3, 2)), jnp.float32),
        "velocity": gaussian(arg_keys[1], (3, NZ, QY, NP), 0.5, 3.0, ((1, 16), (3, 2)), jnp.float32),
        "lumped_mass": jnp.clip(jnp.exp(math.log(3.0) - 2.3025851 * jax.random.uniform(arg_keys[2], (NZ, QY, NP), jnp.float32) ** level_of(arg_keys[2], (NZ, QY, NP), ((0, 16), (2, 2)), -0.2, 0.2)), 0.3, 3.0),
        "plastic_strain": gaussian(arg_keys[3], (3, NF, NZ, QY, NP), 0.2, 1.0, ((2, 16), (4, 2)), jnp.float32),
        "hardening_strain": jnp.clip(jnp.exp(math.log(0.5) - 3.912023 * jax.random.uniform(arg_keys[4], (3, NF, NZ, QY, NP), jnp.float32) ** level_of(arg_keys[4], (3, NF, NZ, QY, NP), ((2, 16), (4, 2)), -0.2, 0.2)), 0.01, 0.5),
        "material_ids": set_ends(jax.random.randint(arg_keys[5], (3, NF, NZ, QY, NP), 0, NMAT), jax.random.fold_in(arg_keys[5], 1), 0, NMAT - 1).astype(jnp.int32),
        "material_table": jnp.clip(jnp.exp(jax.random.uniform(arg_keys[6], (NMAT, 3), jnp.float32, math.log(0.5), math.log(2.0))), 0.5, 2.0),
        "ground_accel": gaussian(arg_keys[7], (STEPS, 3), 1.0, 4.0, (), jnp.float32),
        "snapshot_history": gaussian(arg_keys[8], (HIST, 3, NZ, QY, NP), 1.0, 6.0, ((2, 16), (4, 2))),
        "mode_shapes": draw_mode_shapes(jax.random.fold_in(arg_keys[10], 71), 0),
    }


time_step = 0.3
mass_damping = 0.1
stiff_damping = 0.05
shear_stiff = 0.5
axial_components = (2, 1, 0)

def fibre_props(material_ids, material_table):
    modulus = jnp.zeros(material_ids.shape, jnp.float32)
    yields = jnp.zeros(material_ids.shape, jnp.float32)
    slopes = jnp.zeros(material_ids.shape, jnp.float32)
    for material_index in range(material_table.shape[0]):
        selected = (material_ids == material_index).astype(jnp.float32)
        modulus = modulus + selected * material_table[material_index, 0]
        yields = yields + selected * (0.4 * material_table[material_index, 1])
        slopes = slopes + selected * (0.1 * material_table[material_index, 2])
    return (modulus, yields, slopes)

def bar_update(stretch, stretch_rate, plastic, harden, modulus, yields, slopes, axial_index):
    trial_stress = modulus * (stretch[axial_index][None] - plastic)
    excess = jnp.abs(trial_stress) - (yields + slopes * harden)
    growth = jnp.maximum(excess, 0.0) / (modulus + slopes)
    flow_sign = jnp.sign(trial_stress)
    plastic_new = plastic + growth * flow_sign
    harden_new = harden + growth
    stress = trial_stress - modulus * growth * flow_sign
    axial_force = jnp.mean(stress, axis=0)
    tangent = jnp.mean(modulus, axis=0)
    component_list = []
    for component in range(3):
        if component == axial_index:
            component_list.append(axial_force + stiff_damping * tangent * stretch_rate[component])
        else:
            component_list.append(shear_stiff * (stretch[component] + stiff_damping * stretch_rate[component]))
    return (jnp.stack(component_list), plastic_new, harden_new)

def earlier_of(bar_index, field):
    if bar_index == 0:
        return jnp.concatenate([jnp.zeros_like(field[:, :1]), field[:, :-1]], axis=1)
    if bar_index == 1:
        return jnp.concatenate([jnp.zeros_like(field[:, :, :1]), field[:, :, :-1]], axis=2)
    return jnp.roll(field, 1, axis=3)

def later_of(bar_index, field):
    if bar_index == 0:
        return jnp.concatenate([field[:, 1:], jnp.zeros_like(field[:, :1])], axis=1)
    if bar_index == 1:
        return jnp.concatenate([field[:, :, 1:], jnp.zeros_like(field[:, :, :1])], axis=2)
    return jnp.roll(field, -1, axis=3)

def reference(displacement, velocity, lumped_mass, plastic_strain, hardening_strain, material_ids, material_table, ground_accel, snapshot_history, mode_shapes):
    modulus, yields, slopes = fibre_props(material_ids, material_table)
    disp_now, velo_now = (displacement, velocity)
    plastic_now, harden_now = (plastic_strain, hardening_strain)
    new_snapshots = []
    for step_index in range(STEPS):
        bar_forces, plastic_parts, harden_parts = ([], [], [])
        for bar_index in range(3):
            bar_force, plastic_part, harden_part = bar_update(disp_now - earlier_of(bar_index, disp_now), velo_now - earlier_of(bar_index, velo_now), plastic_now[bar_index], harden_now[bar_index], modulus[bar_index], yields[bar_index], slopes[bar_index], axial_components[bar_index])
            bar_forces.append(bar_force)
            plastic_parts.append(plastic_part)
            harden_parts.append(harden_part)
        plastic_now = jnp.stack(plastic_parts)
        harden_now = jnp.stack(harden_parts)
        resisting = jnp.zeros_like(disp_now)
        for bar_index in range(3):
            resisting = resisting + bar_forces[bar_index] - later_of(bar_index, bar_forces[bar_index])
        acceleration = -ground_accel[step_index][:, None, None, None] - resisting / lumped_mass[None]
        velo_now = ((1.0 - 0.5 * mass_damping * time_step) * velo_now + time_step * acceleration) / (1.0 + 0.5 * mass_damping * time_step)
        disp_now = disp_now + time_step * velo_now
        new_snapshots.append(disp_now.astype(jnp.bfloat16))
    snapshots = jnp.concatenate([snapshot_history, jnp.stack(new_snapshots)], axis=0)

    def accumulate(level_index, carry):
        mass_gram, projected = carry
        modes_level = lax.dynamic_slice_in_dim(mode_shapes, level_index, 1, axis=2)
        mass_level = lax.dynamic_slice_in_dim(lumped_mass, level_index, 1, axis=0)
        snaps_level = lax.dynamic_slice_in_dim(snapshots, level_index, 1, axis=2)
        weighted = (modes_level.astype(jnp.float32) * mass_level[None, None]).astype(jnp.bfloat16).reshape(MODES, -1)
        flat_modes = modes_level.reshape(MODES, -1)
        flat_snaps = snaps_level.reshape(SNAP, -1)
        mass_gram = mass_gram + jnp.dot(weighted.astype(jnp.float32), flat_modes.T.astype(jnp.float32), preferred_element_type=jnp.float32)
        projected = projected + jnp.dot(weighted.astype(jnp.float32), flat_snaps.T.astype(jnp.float32), preferred_element_type=jnp.float32)
        return (mass_gram, projected)
    start_carry = (jnp.zeros((MODES, MODES), jnp.float32), jnp.zeros((MODES, SNAP), jnp.float32))
    mass_gram, projected = lax.fori_loop(0, NZ, accumulate, start_carry)
    factor = jnp.linalg.cholesky(mass_gram)
    modal_coords = jax.scipy.linalg.cho_solve((factor, True), projected)
    return (disp_now, velo_now, plastic_now, harden_now, modal_coords)
```

```python
import functools

import jax
import jax.numpy as jnp
from jax import lax
from jax.experimental import pallas as pl
from jax.experimental.pallas import tpu as pltpu
from jax.sharding import PartitionSpec as P

time_step = 0.3
mass_damping = 0.1
stiff_damping = 0.05
shear_stiff = 0.5
axial_components = (2, 1, 0)
HIGHEST = lax.Precision.HIGHEST
vmem_limit = 48 * 1024 * 1024


def mesh_id(linear, plan):
    return {"height": lax.div(linear, plan), "plan": lax.rem(linear, plan)}


def signal(semaphore, device):
    pl.semaphore_signal(semaphore, inc=1, device_id=device, device_id_type=pl.DeviceIdType.MESH)


def remote(source, target, send_sem, recv_sem, device):
    return pltpu.make_async_remote_copy(
        src_ref=source,
        dst_ref=target,
        send_sem=send_sem,
        recv_sem=recv_sem,
        device_id=device,
        device_id_type=pl.DeviceIdType.MESH,
    )


def greet_all(me, count, plan):
    barrier = pltpu.get_barrier_semaphore()

    def greet(offset, _):
        signal(barrier, mesh_id(lax.rem(me + offset, count), plan))
        return 0

    lax.fori_loop(1, count, greet, 0)
    return barrier


def wait_bytes(ref, semaphore):
    pltpu.make_async_copy(ref, ref, semaphore).wait()


def material_props(ids, table_ref):
    kinds = table_ref.shape[0]
    modulus = jnp.full(ids.shape, table_ref[0, 0], jnp.float32)
    yields = jnp.full(ids.shape, 0.4 * table_ref[0, 1], jnp.float32)
    slopes = jnp.full(ids.shape, 0.1 * table_ref[0, 2], jnp.float32)
    for kind in range(1, kinds):
        chosen = ids == kind
        modulus = jnp.where(chosen, table_ref[kind, 0], modulus)
        yields = jnp.where(chosen, 0.4 * table_ref[kind, 1], yields)
        slopes = jnp.where(chosen, 0.1 * table_ref[kind, 2], slopes)
    return modulus, yields, slopes, 1.0 / (modulus + slopes)


def fibre_step(stretch, plastic, harden, modulus, yields, slopes, inverse):
    trial = modulus * (stretch - plastic)
    excess = jnp.abs(trial) - (yields + slopes * harden)
    growth = jnp.maximum(excess, 0.0) * inverse
    signed = jnp.where(trial < 0.0, -growth, growth)
    return trial - modulus * signed, plastic + signed, harden + growth


def steps_kernel(
    heights, plan,
    disp_in, velo_in, mass_in, plastic_in, harden_in, ids_in, table_ref, accel_ref,
    disp_out, velo_out, plastic_out, harden_out, snaps_out,
    velos, props, top_plastic, top_harden, top_ids, top_props,
    near_disp, near_velo, edge_send, edge_recv,
    disp_send_sem, disp_recv_sem, velo_send_sem, velo_recv_sem, state_send_sem, state_recv_sem,
):
    h, p = lax.axis_index("height"), lax.axis_index("plan")
    fibres = plastic_in.shape[1]
    rows, columns = mass_in.shape
    steps = accel_ref.shape[0]
    has_below, has_above = h > 0, h < heights - 1
    below = {"height": h - 1, "plan": p}
    above = {"height": h + 1, "plan": p}
    left = {"height": h, "plan": lax.rem(p + plan - 1, plan)}
    right = {"height": h, "plan": lax.rem(p + 1, plan)}
    lane = lax.broadcasted_iota(jnp.int32, (rows, columns), 1)
    row = lax.broadcasted_iota(jnp.int32, (rows, columns), 0)
    last = columns - 1

    barrier = pltpu.get_barrier_semaphore()

    @pl.when(has_below)
    def _():
        signal(barrier, below)

    @pl.when(has_above)
    def _():
        signal(barrier, above)

    signal(barrier, left)
    signal(barrier, right)

    velos[0] = velo_in[...]
    packed = [jnp.zeros((rows, columns), jnp.float32) for _ in range(3)]
    for f in range(fibres):
        for part, value in enumerate(
            (plastic_in[2, f], harden_in[2, f], ids_in[2, f].astype(jnp.float32))
        ):
            packed[part] = jnp.where(lane == f, value[:, 0:1], packed[part])
    for part in range(3):
        edge_send[part] = packed[part]

    greetings = 2 + has_below.astype(jnp.int32) + has_above.astype(jnp.int32)
    pl.semaphore_wait(barrier, greetings)

    def disp_copy(side, device):
        return remote(
            disp_in, near_disp.at[side], disp_send_sem.at[side], disp_recv_sem.at[side], device
        )

    def velo_copy(side, step, device):
        return remote(
            velos.at[step], near_velo.at[step, side],
            velo_send_sem.at[step, side], velo_recv_sem.at[step, side], device,
        )

    def state_copies():
        return [
            remote(plastic_in.at[0], top_plastic, state_send_sem.at[0], state_recv_sem.at[0], below),
            remote(harden_in.at[0], top_harden, state_send_sem.at[1], state_recv_sem.at[1], below),
            remote(ids_in.at[0], top_ids, state_send_sem.at[2], state_recv_sem.at[2], below),
        ]

    edge_copy = remote(edge_send, edge_recv, state_send_sem.at[3], state_recv_sem.at[3], left)

    def exchange(step, first):
        copies = [lambda s, d: velo_copy(s, step, d)]
        if first:
            copies.append(disp_copy)

        @pl.when(has_above)
        def _():
            for make in copies:
                make(0, above).start()

        @pl.when(has_below)
        def _():
            for make in copies:
                make(1, below).start()

        for make in copies:
            make(2, right).start()
            make(3, left).start()

    def finish(step, first):
        copies = [lambda s, d: velo_copy(s, step, d)]
        if first:
            copies.append(disp_copy)

        @pl.when(has_below)
        def _():
            for make in copies:
                make(0, below).wait_recv()
                make(1, below).wait_send()

        @pl.when(has_above)
        def _():
            for make in copies:
                make(1, above).wait_recv()
                make(0, above).wait_send()

        for make in copies:
            for side, device in ((2, right), (3, left)):
                make(side, device).wait()

    exchange(0, True)
    edge_copy.start()

    @pl.when(has_below)
    def _():
        for copy in state_copies():
            copy.start()

    @pl.when(jnp.logical_not(has_below))
    def _():
        near_disp[0] = jnp.zeros(near_disp.shape[1:], jnp.float32)
        for step in range(steps):
            near_velo[step, 0] = jnp.zeros(near_velo.shape[2:], jnp.float32)

    @pl.when(jnp.logical_not(has_above))
    def _():
        near_disp[1] = jnp.zeros(near_disp.shape[1:], jnp.float32)
        for step in range(steps):
            near_velo[step, 1] = jnp.zeros(near_velo.shape[2:], jnp.float32)
        top_plastic[...] = jnp.zeros(top_plastic.shape, jnp.float32)
        top_harden[...] = jnp.zeros(top_harden.shape, jnp.float32)
        top_ids[...] = jnp.zeros(top_ids.shape, jnp.int32)

    zero = jnp.zeros((rows, columns), jnp.float32)

    def own_props(f, sums):
        new_sums = []
        for b in range(3):
            found = material_props(ids_in[b, f], table_ref)
            for part in range(4):
                props[part, b, f] = found[part]
            new_sums.append(sums[b] + found[0])
        return tuple(new_sums)

    sums = lax.fori_loop(0, fibres, own_props, (zero, zero, zero))
    tangents = [total * (1.0 / fibres) for total in sums]

    finish(0, True)
    edge_copy.wait()

    @pl.when(has_below)
    def _():
        for copy in state_copies():
            copy.wait_send()

    @pl.when(has_above)
    def _():
        for copy in state_copies():
            copy.wait_recv()

    def above_props(f, total):
        found = material_props(top_ids[f], table_ref)
        for part in range(4):
            top_props[part, f] = found[part]
        return total + found[0]

    top_tangent = lax.fori_loop(0, fibres, above_props, zero) * (1.0 / fibres)

    in_edge = lane < fibres
    edge_plastic, edge_harden = edge_recv[0], edge_recv[1]
    edge_found = material_props(edge_recv[2].astype(jnp.int32), table_ref)

    def edge_mean(value):
        return jnp.sum(jnp.where(in_edge, value, 0.0), axis=1, keepdims=True) * (1.0 / fibres)

    edge_tangent = edge_mean(edge_found[0])

    disp = [disp_in[c] for c in range(3)]
    velo = [velo_in[c] for c in range(3)]
    mass_inverse = 1.0 / mass_in[...]

    def rows_before(x):
        return jnp.where(row == 0, 0.0, pltpu.roll(x, 1, 0))

    def rows_after(x):
        return jnp.where(row == rows - 1, 0.0, pltpu.roll(x, rows - 1, 0))

    def rim_before(x, left_block):
        return pltpu.roll(jnp.where(lane == last, left_block, x), 1, 1)

    def shear(stretch, rate):
        return shear_stiff * (stretch + stiff_damping * rate)

    for step in range(steps):
        if step > 0:
            finish(step, False)
            for side in range(4):
                for c in range(3):
                    near_disp[side, c] = near_disp[side, c] + time_step * near_velo[step, side, c]
        source_plastic, source_harden = (
            (plastic_in, harden_in) if step == 0 else (plastic_out, harden_out)
        )
        stretch = [
            [disp[c] - near_disp[0, c] for c in range(3)],
            [disp[c] - rows_before(disp[c]) for c in range(3)],
            [disp[c] - rim_before(disp[c], near_disp[2, c]) for c in range(3)],
        ]
        rate = [
            [velo[c] - near_velo[step, 0, c] for c in range(3)],
            [velo[c] - rows_before(velo[c]) for c in range(3)],
            [velo[c] - rim_before(velo[c], near_velo[step, 2, c]) for c in range(3)],
        ]
        top_stretch = [near_disp[1, c] - disp[c] for c in range(3)]
        top_rate = [near_velo[step, 1, c] - velo[c] for c in range(3)]
        rim_stretch = [near_disp[3, c][:, 0:1] - disp[c][:, last:] for c in range(3)]
        rim_rate = [near_velo[step, 3, c][:, 0:1] - velo[c][:, last:] for c in range(3)]

        def fibre(f, totals):
            new_totals = []
            for b in range(3):
                stress, plastic, harden = fibre_step(
                    stretch[b][axial_components[b]], source_plastic[b, f], source_harden[b, f],
                    props[0, b, f], props[1, b, f], props[2, b, f], props[3, b, f],
                )
                plastic_out[b, f] = plastic
                harden_out[b, f] = harden
                new_totals.append(totals[b] + stress)
            stress, plastic, harden = fibre_step(
                top_stretch[axial_components[0]], top_plastic[f], top_harden[f],
                top_props[0, f], top_props[1, f], top_props[2, f], top_props[3, f],
            )
            top_plastic[f] = plastic
            top_harden[f] = harden
            new_totals.append(totals[3] + stress)
            return tuple(new_totals)

        totals = lax.fori_loop(0, fibres, fibre, (zero, zero, zero, zero))
        edge_stress, edge_plastic, edge_harden = fibre_step(
            rim_stretch[axial_components[2]], edge_plastic, edge_harden, *edge_found
        )
        edge_axial = edge_mean(edge_stress)

        new_velo = []
        for c in range(3):
            force = []
            for b in range(3):
                if c == axial_components[b]:
                    force.append(
                        totals[b] * (1.0 / fibres) + stiff_damping * tangents[b] * rate[b][c]
                    )
                else:
                    force.append(shear(stretch[b][c], rate[b][c]))
            if c == axial_components[0]:
                top = totals[3] * (1.0 / fibres) + stiff_damping * top_tangent * top_rate[c]
            else:
                top = shear(top_stretch[c], top_rate[c])
            if c == axial_components[2]:
                rim = edge_axial + stiff_damping * edge_tangent * rim_rate[c]
            else:
                rim = shear(rim_stretch[c], rim_rate[c])
            top = jnp.where(has_above, top, 0.0)
            after_rim = jnp.where(lane == last, rim, pltpu.roll(force[2], last, 1))
            resisting = (
                force[0] - top + (force[1] - rows_after(force[1])) + (force[2] - after_rim)
            )
            acceleration = -accel_ref[step, c] - resisting * mass_inverse
            new_velo.append(
                ((1.0 - 0.5 * mass_damping * time_step) * velo[c] + time_step * acceleration)
                * (1.0 / (1.0 + 0.5 * mass_damping * time_step))
            )
        velo = new_velo
        if step + 1 < steps:
            for c in range(3):
                velos[step + 1, c] = velo[c]
            exchange(step + 1, False)
        for c in range(3):
            disp[c] = disp[c] + time_step * velo[c]
            snaps_out[step, c] = disp[c].astype(jnp.bfloat16)
    for c in range(3):
        disp_out[c] = disp[c]
        velo_out[c] = velo[c]


def run_steps(disp, velo, mass, plastic, harden, ids, table, accel):
    heights, plan = lax.axis_size("height"), lax.axis_size("plan")
    steps = accel.shape[0]
    vmem = pl.BlockSpec(memory_space=pltpu.VMEM)
    smem = pl.BlockSpec(memory_space=pltpu.SMEM)
    f32 = jnp.float32
    fibres = plastic.shape[1]
    plane = mass.shape
    return pl.pallas_call(
        functools.partial(steps_kernel, heights, plan),
        out_shape=(
            jax.ShapeDtypeStruct(disp.shape, f32),
            jax.ShapeDtypeStruct(velo.shape, f32),
            jax.ShapeDtypeStruct(plastic.shape, f32),
            jax.ShapeDtypeStruct(harden.shape, f32),
            jax.ShapeDtypeStruct((steps,) + disp.shape, jnp.bfloat16),
        ),
        in_specs=[vmem] * 6 + [smem] * 2,
        out_specs=(vmem,) * 5,
        scratch_shapes=[
            pltpu.VMEM((steps,) + velo.shape, f32),
            pltpu.VMEM((4,) + plastic.shape, f32),
            pltpu.VMEM((fibres,) + plane, f32),
            pltpu.VMEM((fibres,) + plane, f32),
            pltpu.VMEM((fibres,) + plane, jnp.int32),
            pltpu.VMEM((4, fibres) + plane, f32),
            pltpu.VMEM((4,) + disp.shape, f32),
            pltpu.VMEM((steps, 4) + velo.shape, f32),
            pltpu.VMEM((3,) + plane, f32),
            pltpu.VMEM((3,) + plane, f32),
            pltpu.SemaphoreType.DMA((4,)),
            pltpu.SemaphoreType.DMA((4,)),
            pltpu.SemaphoreType.DMA((steps, 4)),
            pltpu.SemaphoreType.DMA((steps, 4)),
            pltpu.SemaphoreType.DMA((4,)),
            pltpu.SemaphoreType.DMA((4,)),
        ],
        compiler_params=pltpu.CompilerParams(
            collective_id=0, has_side_effects=True, vmem_limit_bytes=vmem_limit
        ),
        name="time_steps",
    )(disp, velo, mass, plastic, harden, ids, table, accel)


def gram_kernel(
    count, plan, part_ref, out_ref, landed, total, send_sem, recv_sem, give_sem, take_sem
):
    me = lax.axis_index("height") * plan + lax.axis_index("plan")
    barrier = greet_all(me, count, plan)
    pl.semaphore_wait(barrier, count - 1)

    def send(offset, _):
        target = lax.rem(me + offset, count)
        remote(
            part_ref.at[target], landed.at[offset - 1], send_sem, recv_sem, mesh_id(target, plan)
        ).start()
        return 0

    lax.fori_loop(1, count, send, 0)
    wait_bytes(landed, recv_sem)
    total[...] = part_ref[me] + jnp.sum(landed[...], axis=0)

    def give(offset, _):
        target = lax.rem(me + offset, count)
        remote(total, out_ref.at[me], give_sem, take_sem, mesh_id(target, plan)).start()
        return 0

    lax.fori_loop(1, count, give, 0)
    out_ref[me] = total[...]
    wait_bytes(landed, take_sem)
    wait_bytes(landed, send_sem)
    wait_bytes(landed, give_sem)


def gram_total(part):
    plan = lax.axis_size("plan")
    count = lax.axis_size(("height", "plan"))
    modes = part.shape[0]
    rows = modes // count
    vmem = pl.BlockSpec(memory_space=pltpu.VMEM)
    out = pl.pallas_call(
        functools.partial(gram_kernel, count, plan),
        out_shape=jax.ShapeDtypeStruct((count, rows, modes), jnp.float32),
        in_specs=[vmem],
        out_specs=vmem,
        scratch_shapes=[
            pltpu.VMEM((count - 1, rows, modes), jnp.float32),
            pltpu.VMEM((rows, modes), jnp.float32),
        ] + [pltpu.SemaphoreType.DMA] * 4,
        compiler_params=pltpu.CompilerParams(
            collective_id=1, has_side_effects=True, vmem_limit_bytes=vmem_limit
        ),
        name="gram_sum",
    )(part.reshape(count, rows, modes))
    return out.reshape(modes, modes)


def coords_kernel(count, plan, part_ref, out_ref, landed, send_sem, recv_sem):
    me = lax.axis_index("height") * plan + lax.axis_index("plan")
    barrier = greet_all(me, count, plan)
    pl.semaphore_wait(barrier, count - 1)

    def send(offset, _):
        target = lax.rem(me + offset, count)
        remote(
            part_ref.at[target], landed.at[offset - 1], send_sem, recv_sem, mesh_id(target, plan)
        ).start()
        return 0

    lax.fori_loop(1, count, send, 0)
    wait_bytes(landed, recv_sem)
    out_ref[...] = part_ref[me] + jnp.sum(landed[...], axis=0)
    wait_bytes(landed, send_sem)


def coords_total(part):
    plan = lax.axis_size("plan")
    count = lax.axis_size(("height", "plan"))
    modes, snaps = part.shape
    rows = modes // count
    vmem = pl.BlockSpec(memory_space=pltpu.VMEM)
    return pl.pallas_call(
        functools.partial(coords_kernel, count, plan),
        out_shape=jax.ShapeDtypeStruct((rows, snaps), jnp.float32),
        in_specs=[vmem],
        out_specs=vmem,
        scratch_shapes=[pltpu.VMEM((count - 1, rows, snaps), jnp.float32)]
        + [pltpu.SemaphoreType.DMA] * 2,
        compiler_params=pltpu.CompilerParams(
            collective_id=2, has_side_effects=True, vmem_limit_bytes=vmem_limit
        ),
        name="coords_sum",
    )(part.reshape(count, rows, snaps))


def solve_kernel(gram_ref, projected_ref, out_ref):
    modes = gram_ref.shape[0]
    row = lax.broadcasted_iota(jnp.int32, (modes, modes), 0)
    column = lax.broadcasted_iota(jnp.int32, (modes, modes), 1)
    lower = jnp.where(row >= column, gram_ref[...], 0.0)
    gram = lower + jnp.where(row == column, 0.0, lower).T
    identity = jnp.where(row == column, 1.0, 0.0)
    size = jnp.max(jnp.sum(jnp.abs(gram), axis=1))
    guess = identity * (1.0 / size)

    def multiply(a, b):
        return jnp.dot(a, b, precision=HIGHEST, preferred_element_type=jnp.float32)

    def unfinished(state):
        turns, error, _ = state
        return jnp.logical_and(turns < 60, error > 1e-3)

    def improve(state):
        turns, _, inverse = state
        residual = identity - multiply(gram, inverse)
        error = jnp.max(jnp.sum(jnp.abs(residual), axis=0))
        return turns + 1, error, inverse + multiply(inverse, residual)

    _, _, inverse = lax.while_loop(unfinished, improve, (0, jnp.float32(2.0), guess))
    out_ref[...] = multiply(inverse, projected_ref[...])


def solve(gram, projected):
    vmem = pl.BlockSpec(memory_space=pltpu.VMEM)
    return pl.pallas_call(
        solve_kernel,
        out_shape=jax.ShapeDtypeStruct(projected.shape, jnp.float32),
        in_specs=[vmem, vmem],
        out_specs=vmem,
        compiler_params=pltpu.CompilerParams(vmem_limit_bytes=vmem_limit),
        name="solve",
    )(gram, projected)


def body(
    displacement,
    velocity,
    lumped_mass,
    plastic_strain,
    hardening_strain,
    material_ids,
    material_table,
    ground_accel,
    snapshot_history,
    mode_shapes,
):
    mode_count = mode_shapes.shape[0]
    flat_modes = mode_shapes.reshape(mode_count, -1)
    weighted = (
        (mode_shapes.astype(jnp.float32) * lumped_mass[None, None])
        .astype(jnp.bfloat16)
        .reshape(mode_count, -1)
    )
    contract_last = (((1,), (1,)), ((), ()))
    mass_gram = lax.dot_general(
        weighted, flat_modes, contract_last, preferred_element_type=jnp.float32
    )
    flat_history = snapshot_history.reshape(snapshot_history.shape[0], -1)
    projected_history = lax.dot_general(
        weighted, flat_history, contract_last, preferred_element_type=jnp.float32
    )
    gram = gram_total(mass_gram)
    disp_end, velo_end, plastic_end, harden_end, new_snaps = run_steps(
        displacement[:, 0], velocity[:, 0], lumped_mass[0], plastic_strain[:, :, 0],
        hardening_strain[:, :, 0], material_ids[:, :, 0], material_table, ground_accel,
    )
    projected_new = lax.dot_general(
        weighted, new_snaps.reshape(new_snaps.shape[0], -1), contract_last,
        preferred_element_type=jnp.float32,
    )
    projected = jnp.concatenate([projected_history, projected_new], axis=1)
    modal_coords = coords_total(solve(gram, projected))
    return (
        disp_end[:, None], velo_end[:, None], plastic_end[:, :, None], harden_end[:, :, None],
        modal_coords,
    )


def solution(mesh):
    return jax.shard_map(
        body,
        mesh=mesh,
        in_specs=(
            P(None, "height", None, "plan"),
            P(None, "height", None, "plan"),
            P("height", None, "plan"),
            P(None, None, "height", None, "plan"),
            P(None, None, "height", None, "plan"),
            P(None, None, "height", None, "plan"),
            P(),
            P(),
            P(None, None, "height", None, "plan"),
            P(None, None, "height", None, "plan"),
        ),
        out_specs=(
            P(None, "height", None, "plan"),
            P(None, "height", None, "plan"),
            P(None, None, "height", None, "plan"),
            P(None, None, "height", None, "plan"),
            P(("height", "plan"), None),
        ),
        check_vma=False,
    )
```

```python
import functools
import math

import jax
import jax.numpy as jnp
from jax import lax
from jax.experimental import pallas as pl
from jax.experimental.pallas import tpu as pltpu
from jax.sharding import PartitionSpec as P

time_step = 0.3
mass_damping = 0.1
stiff_damping = 0.05
shear_stiff = 0.5
axial_components = (2, 1, 0)
HIGHEST = lax.Precision.HIGHEST
vmem_limit = 48 * 1024 * 1024


def mesh_id(linear, plan):
    return {"height": lax.div(linear, plan), "plan": lax.rem(linear, plan)}


def signal(semaphore, device):
    pl.semaphore_signal(semaphore, inc=1, device_id=device, device_id_type=pl.DeviceIdType.MESH)


def remote(source, target, send_sem, recv_sem, device):
    return pltpu.make_async_remote_copy(
        src_ref=source,
        dst_ref=target,
        send_sem=send_sem,
        recv_sem=recv_sem,
        device_id=device,
        device_id_type=pl.DeviceIdType.MESH,
    )


def greet_all(me, count, plan):
    barrier = pltpu.get_barrier_semaphore()

    def greet(offset, _):
        signal(barrier, mesh_id(lax.rem(me + offset, count), plan))
        return 0

    lax.fori_loop(1, count, greet, 0)
    return barrier


def wait_bytes(ref, semaphore):
    pltpu.make_async_copy(ref, ref, semaphore).wait()


def material_props(ids, table_ref):
    kinds = table_ref.shape[0]
    modulus = jnp.full(ids.shape, table_ref[0, 0], jnp.float32)
    yields = jnp.full(ids.shape, 0.4 * table_ref[0, 1], jnp.float32)
    slopes = jnp.full(ids.shape, 0.1 * table_ref[0, 2], jnp.float32)
    for kind in range(1, kinds):
        chosen = ids == kind
        modulus = jnp.where(chosen, table_ref[kind, 0], modulus)
        yields = jnp.where(chosen, 0.4 * table_ref[kind, 1], yields)
        slopes = jnp.where(chosen, 0.1 * table_ref[kind, 2], slopes)
    return modulus, yields, slopes, 1.0 / (modulus + slopes)


def fibre_step(stretch, plastic, harden, modulus, yields, slopes, inverse):
    trial = modulus * (stretch - plastic)
    excess = jnp.abs(trial) - (yields + slopes * harden)
    growth = jnp.maximum(excess, 0.0) * inverse
    signed = jnp.where(trial < 0.0, -growth, growth)
    return trial - modulus * signed, plastic + signed, harden + growth


def steps_kernel(
    heights, plan,
    disp_in, velo_in, mass_in, plastic_in, harden_in, ids_in, table_ref, accel_ref,
    disp_out, velo_out, plastic_out, harden_out, snaps_out,
    velos, props, top_plastic, top_harden, top_ids, top_props,
    near_disp, near_velo, edge_send, edge_recv,
    disp_send_sem, disp_recv_sem, velo_send_sem, velo_recv_sem, state_send_sem, state_recv_sem,
):
    h, p = lax.axis_index("height"), lax.axis_index("plan")
    fibres = plastic_in.shape[1]
    rows, columns = mass_in.shape
    steps = accel_ref.shape[0]
    has_below, has_above = h > 0, h < heights - 1
    below = {"height": h - 1, "plan": p}
    above = {"height": h + 1, "plan": p}
    left = {"height": h, "plan": lax.rem(p + plan - 1, plan)}
    right = {"height": h, "plan": lax.rem(p + 1, plan)}
    lane = lax.broadcasted_iota(jnp.int32, (rows, columns), 1)
    row = lax.broadcasted_iota(jnp.int32, (rows, columns), 0)
    last = columns - 1

    barrier = pltpu.get_barrier_semaphore()

    @pl.when(has_below)
    def _():
        signal(barrier, below)

    @pl.when(has_above)
    def _():
        signal(barrier, above)

    signal(barrier, left)
    signal(barrier, right)

    velos[0] = velo_in[...]
    packed = [jnp.zeros((rows, columns), jnp.float32) for _ in range(3)]
    for f in range(fibres):
        for part, value in enumerate(
            (plastic_in[2, f], harden_in[2, f], ids_in[2, f].astype(jnp.float32))
        ):
            packed[part] = jnp.where(lane == f, value[:, 0:1], packed[part])
    for part in range(3):
        edge_send[part] = packed[part]

    greetings = 2 + has_below.astype(jnp.int32) + has_above.astype(jnp.int32)
    pl.semaphore_wait(barrier, greetings)

    def disp_copy(side, device):
        return remote(
            disp_in, near_disp.at[side], disp_send_sem.at[side], disp_recv_sem.at[side], device
        )

    def velo_copy(side, step, device):
        return remote(
            velos.at[step], near_velo.at[step, side],
            velo_send_sem.at[step, side], velo_recv_sem.at[step, side], device,
        )

    def state_copies():
        return [
            remote(plastic_in.at[0], top_plastic, state_send_sem.at[0], state_recv_sem.at[0], below),
            remote(harden_in.at[0], top_harden, state_send_sem.at[1], state_recv_sem.at[1], below),
            remote(ids_in.at[0], top_ids, state_send_sem.at[2], state_recv_sem.at[2], below),
        ]

    edge_copy = remote(edge_send, edge_recv, state_send_sem.at[3], state_recv_sem.at[3], left)

    def exchange(step, first):
        copies = [lambda s, d: velo_copy(s, step, d)]
        if first:
            copies.append(disp_copy)

        @pl.when(has_above)
        def _():
            for make in copies:
                make(0, above).start()

        @pl.when(has_below)
        def _():
            for make in copies:
                make(1, below).start()

        for make in copies:
            make(2, right).start()
            make(3, left).start()

    def finish(step, first):
        copies = [lambda s, d: velo_copy(s, step, d)]
        if first:
            copies.append(disp_copy)

        @pl.when(has_below)
        def _():
            for make in copies:
                make(0, below).wait_recv()
                make(1, below).wait_send()

        @pl.when(has_above)
        def _():
            for make in copies:
                make(1, above).wait_recv()
                make(0, above).wait_send()

        for make in copies:
            for side, device in ((2, right), (3, left)):
                make(side, device).wait()

    exchange(0, True)
    edge_copy.start()

    @pl.when(has_below)
    def _():
        for copy in state_copies():
            copy.start()

    @pl.when(jnp.logical_not(has_below))
    def _():
        near_disp[0] = jnp.zeros(near_disp.shape[1:], jnp.float32)
        for step in range(steps):
            near_velo[step, 0] = jnp.zeros(near_velo.shape[2:], jnp.float32)

    @pl.when(jnp.logical_not(has_above))
    def _():
        near_disp[1] = jnp.zeros(near_disp.shape[1:], jnp.float32)
        for step in range(steps):
            near_velo[step, 1] = jnp.zeros(near_velo.shape[2:], jnp.float32)
        top_plastic[...] = jnp.zeros(top_plastic.shape, jnp.float32)
        top_harden[...] = jnp.zeros(top_harden.shape, jnp.float32)
        top_ids[...] = jnp.zeros(top_ids.shape, jnp.int32)

    zero = jnp.zeros((rows, columns), jnp.float32)

    def own_props(f, sums):
        new_sums = []
        for b in range(3):
            found = material_props(ids_in[b, f], table_ref)
            for part in range(4):
                props[part, b, f] = found[part]
            new_sums.append(sums[b] + found[0])
        return tuple(new_sums)

    sums = lax.fori_loop(0, fibres, own_props, (zero, zero, zero))
    tangents = [total * (1.0 / fibres) for total in sums]

    finish(0, True)
    edge_copy.wait()

    @pl.when(has_below)
    def _():
        for copy in state_copies():
            copy.wait_send()

    @pl.when(has_above)
    def _():
        for copy in state_copies():
            copy.wait_recv()

    def above_props(f, total):
        found = material_props(top_ids[f], table_ref)
        for part in range(4):
            top_props[part, f] = found[part]
        return total + found[0]

    top_tangent = lax.fori_loop(0, fibres, above_props, zero) * (1.0 / fibres)

    in_edge = lane < fibres
    edge_plastic, edge_harden = edge_recv[0], edge_recv[1]
    edge_found = material_props(edge_recv[2].astype(jnp.int32), table_ref)

    def edge_mean(value):
        return jnp.sum(jnp.where(in_edge, value, 0.0), axis=1, keepdims=True) * (1.0 / fibres)

    edge_tangent = edge_mean(edge_found[0])

    disp = [disp_in[c] for c in range(3)]
    velo = [velo_in[c] for c in range(3)]
    mass_inverse = 1.0 / mass_in[...]

    def rows_before(x):
        return jnp.where(row == 0, 0.0, pltpu.roll(x, 1, 0))

    def rows_after(x):
        return jnp.where(row == rows - 1, 0.0, pltpu.roll(x, rows - 1, 0))

    def rim_before(x, left_block):
        return pltpu.roll(jnp.where(lane == last, left_block, x), 1, 1)

    def shear(stretch, rate):
        return shear_stiff * (stretch + stiff_damping * rate)

    for step in range(steps):
        if step > 0:
            finish(step, False)
            for side in range(4):
                for c in range(3):
                    near_disp[side, c] = near_disp[side, c] + time_step * near_velo[step, side, c]
        source_plastic, source_harden = (
            (plastic_in, harden_in) if step == 0 else (plastic_out, harden_out)
        )
        stretch = [
            [disp[c] - near_disp[0, c] for c in range(3)],
            [disp[c] - rows_before(disp[c]) for c in range(3)],
            [disp[c] - rim_before(disp[c], near_disp[2, c]) for c in range(3)],
        ]
        rate = [
            [velo[c] - near_velo[step, 0, c] for c in range(3)],
            [velo[c] - rows_before(velo[c]) for c in range(3)],
            [velo[c] - rim_before(velo[c], near_velo[step, 2, c]) for c in range(3)],
        ]
        top_stretch = [near_disp[1, c] - disp[c] for c in range(3)]
        top_rate = [near_velo[step, 1, c] - velo[c] for c in range(3)]
        rim_stretch = [near_disp[3, c][:, 0:1] - disp[c][:, last:] for c in range(3)]
        rim_rate = [near_velo[step, 3, c][:, 0:1] - velo[c][:, last:] for c in range(3)]

        def fibre(f, totals):
            new_totals = []
            for b in range(3):
                stress, plastic, harden = fibre_step(
                    stretch[b][axial_components[b]], source_plastic[b, f], source_harden[b, f],
                    props[0, b, f], props[1, b, f], props[2, b, f], props[3, b, f],
                )
                plastic_out[b, f] = plastic
                harden_out[b, f] = harden
                new_totals.append(totals[b] + stress)
            stress, plastic, harden = fibre_step(
                top_stretch[axial_components[0]], top_plastic[f], top_harden[f],
                top_props[0, f], top_props[1, f], top_props[2, f], top_props[3, f],
            )
            top_plastic[f] = plastic
            top_harden[f] = harden
            new_totals.append(totals[3] + stress)
            return tuple(new_totals)

        totals = lax.fori_loop(0, fibres, fibre, (zero, zero, zero, zero))
        edge_stress, edge_plastic, edge_harden = fibre_step(
            rim_stretch[axial_components[2]], edge_plastic, edge_harden, *edge_found
        )
        edge_axial = edge_mean(edge_stress)

        new_velo = []
        for c in range(3):
            force = []
            for b in range(3):
                if c == axial_components[b]:
                    force.append(
                        totals[b] * (1.0 / fibres) + stiff_damping * tangents[b] * rate[b][c]
                    )
                else:
                    force.append(shear(stretch[b][c], rate[b][c]))
            if c == axial_components[0]:
                top = totals[3] * (1.0 / fibres) + stiff_damping * top_tangent * top_rate[c]
            else:
                top = shear(top_stretch[c], top_rate[c])
            if c == axial_components[2]:
                rim = edge_axial + stiff_damping * edge_tangent * rim_rate[c]
            else:
                rim = shear(rim_stretch[c], rim_rate[c])
            top = jnp.where(has_above, top, 0.0)
            after_rim = jnp.where(lane == last, rim, pltpu.roll(force[2], last, 1))
            resisting = (
                force[0] - top + (force[1] - rows_after(force[1])) + (force[2] - after_rim)
            )
            acceleration = -accel_ref[step, c] - resisting * mass_inverse
            new_velo.append(
                ((1.0 - 0.5 * mass_damping * time_step) * velo[c] + time_step * acceleration)
                * (1.0 / (1.0 + 0.5 * mass_damping * time_step))
            )
        velo = new_velo
        if step + 1 < steps:
            for c in range(3):
                velos[step + 1, c] = velo[c]
            exchange(step + 1, False)
        for c in range(3):
            disp[c] = disp[c] + time_step * velo[c]
            snaps_out[step, c] = disp[c].astype(jnp.bfloat16)
    for c in range(3):
        disp_out[c] = disp[c]
        velo_out[c] = velo[c]


def run_steps(disp, velo, mass, plastic, harden, ids, table, accel):
    heights, plan = lax.axis_size("height"), lax.axis_size("plan")
    steps = accel.shape[0]
    vmem = pl.BlockSpec(memory_space=pltpu.VMEM)
    smem = pl.BlockSpec(memory_space=pltpu.SMEM)
    f32 = jnp.float32
    fibres = plastic.shape[1]
    plane = mass.shape
    return pl.pallas_call(
        functools.partial(steps_kernel, heights, plan),
        out_shape=(
            jax.ShapeDtypeStruct(disp.shape, f32),
            jax.ShapeDtypeStruct(velo.shape, f32),
            jax.ShapeDtypeStruct(plastic.shape, f32),
            jax.ShapeDtypeStruct(harden.shape, f32),
            jax.ShapeDtypeStruct((steps,) + disp.shape, jnp.bfloat16),
        ),
        in_specs=[vmem] * 6 + [smem] * 2,
        out_specs=(vmem,) * 5,
        scratch_shapes=[
            pltpu.VMEM((steps,) + velo.shape, f32),
            pltpu.VMEM((4,) + plastic.shape, f32),
            pltpu.VMEM((fibres,) + plane, f32),
            pltpu.VMEM((fibres,) + plane, f32),
            pltpu.VMEM((fibres,) + plane, jnp.int32),
            pltpu.VMEM((4, fibres) + plane, f32),
            pltpu.VMEM((4,) + disp.shape, f32),
            pltpu.VMEM((steps, 4) + velo.shape, f32),
            pltpu.VMEM((3,) + plane, f32),
            pltpu.VMEM((3,) + plane, f32),
            pltpu.SemaphoreType.DMA((4,)),
            pltpu.SemaphoreType.DMA((4,)),
            pltpu.SemaphoreType.DMA((steps, 4)),
            pltpu.SemaphoreType.DMA((steps, 4)),
            pltpu.SemaphoreType.DMA((4,)),
            pltpu.SemaphoreType.DMA((4,)),
        ],
        compiler_params=pltpu.CompilerParams(
            collective_id=0, has_side_effects=True, vmem_limit_bytes=vmem_limit
        ),
        name="time_steps",
    )(disp, velo, mass, plastic, harden, ids, table, accel)


def gram_kernel(
    count, plan, part_ref, out_ref, landed, total, send_sem, recv_sem, give_sem, take_sem
):
    me = lax.axis_index("height") * plan + lax.axis_index("plan")
    barrier = greet_all(me, count, plan)
    pl.semaphore_wait(barrier, count - 1)

    def send(offset, _):
        target = lax.rem(me + offset, count)
        remote(
            part_ref.at[target], landed.at[offset - 1], send_sem, recv_sem, mesh_id(target, plan)
        ).start()
        return 0

    lax.fori_loop(1, count, send, 0)
    wait_bytes(landed, recv_sem)
    total[...] = part_ref[me] + jnp.sum(landed[...], axis=0)

    def give(offset, _):
        target = lax.rem(me + offset, count)
        remote(total, out_ref.at[me], give_sem, take_sem, mesh_id(target, plan)).start()
        return 0

    lax.fori_loop(1, count, give, 0)
    out_ref[me] = total[...]
    wait_bytes(landed, take_sem)
    wait_bytes(landed, send_sem)
    wait_bytes(landed, give_sem)


def gram_total(part):
    plan = lax.axis_size("plan")
    count = lax.axis_size(("height", "plan"))
    modes = part.shape[0]
    rows = modes // count
    vmem = pl.BlockSpec(memory_space=pltpu.VMEM)
    out = pl.pallas_call(
        functools.partial(gram_kernel, count, plan),
        out_shape=jax.ShapeDtypeStruct((count, rows, modes), jnp.float32),
        in_specs=[vmem],
        out_specs=vmem,
        scratch_shapes=[
            pltpu.VMEM((count - 1, rows, modes), jnp.float32),
            pltpu.VMEM((rows, modes), jnp.float32),
        ] + [pltpu.SemaphoreType.DMA] * 4,
        compiler_params=pltpu.CompilerParams(
            collective_id=1, has_side_effects=True, vmem_limit_bytes=vmem_limit
        ),
        name="gram_sum",
    )(part.reshape(count, rows, modes))
    return out.reshape(modes, modes)


def coords_kernel(count, plan, part_ref, out_ref, landed, send_sem, recv_sem):
    me = lax.axis_index("height") * plan + lax.axis_index("plan")
    barrier = greet_all(me, count, plan)
    pl.semaphore_wait(barrier, count - 1)

    def send(offset, _):
        target = lax.rem(me + offset, count)
        remote(
            part_ref.at[target], landed.at[offset - 1], send_sem, recv_sem, mesh_id(target, plan)
        ).start()
        return 0

    lax.fori_loop(1, count, send, 0)
    wait_bytes(landed, recv_sem)
    out_ref[...] = part_ref[me] + jnp.sum(landed[...], axis=0)
    wait_bytes(landed, send_sem)


def coords_total(part):
    plan = lax.axis_size("plan")
    count = lax.axis_size(("height", "plan"))
    modes, snaps = part.shape
    rows = modes // count
    vmem = pl.BlockSpec(memory_space=pltpu.VMEM)
    return pl.pallas_call(
        functools.partial(coords_kernel, count, plan),
        out_shape=jax.ShapeDtypeStruct((rows, snaps), jnp.float32),
        in_specs=[vmem],
        out_specs=vmem,
        scratch_shapes=[pltpu.VMEM((count - 1, rows, snaps), jnp.float32)]
        + [pltpu.SemaphoreType.DMA] * 2,
        compiler_params=pltpu.CompilerParams(
            collective_id=2, has_side_effects=True, vmem_limit_bytes=vmem_limit
        ),
        name="coords_sum",
    )(part.reshape(count, rows, snaps))


def solve_kernel(gram_ref, projected_ref, out_ref):
    modes = gram_ref.shape[0]
    row = lax.broadcasted_iota(jnp.int32, (modes, modes), 0)
    column = lax.broadcasted_iota(jnp.int32, (modes, modes), 1)
    lower = jnp.where(row >= column, gram_ref[...], 0.0)
    gram = lower + jnp.where(row == column, 0.0, lower).T
    identity = jnp.where(row == column, 1.0, 0.0)
    size = jnp.max(jnp.sum(jnp.abs(gram), axis=1))
    guess = identity * (1.0 / size)

    def multiply(a, b):
        return jnp.dot(a, b, precision=HIGHEST, preferred_element_type=jnp.float32)

    def unfinished(state):
        turns, error, _ = state
        return jnp.logical_and(turns < 60, error > 1e-3)

    def improve(state):
        turns, _, inverse = state
        residual = identity - multiply(gram, inverse)
        error = jnp.max(jnp.sum(jnp.abs(residual), axis=0))
        return turns + 1, error, inverse + multiply(inverse, residual)

    _, _, inverse = lax.while_loop(unfinished, improve, (0, jnp.float32(2.0), guess))
    out_ref[...] = multiply(inverse, projected_ref[...])


def solve(gram, projected):
    vmem = pl.BlockSpec(memory_space=pltpu.VMEM)
    return pl.pallas_call(
        solve_kernel,
        out_shape=jax.ShapeDtypeStruct(projected.shape, jnp.float32),
        in_specs=[vmem, vmem],
        out_specs=vmem,
        compiler_params=pltpu.CompilerParams(vmem_limit_bytes=vmem_limit),
        name="solve",
    )(gram, projected)


def products_kernel(
    modes_ref, mass_ref, history_ref, recent_ref, gram_ref, projected_ref, modes_wide, snaps_wide
):
    modes, rows, columns = modes_ref.shape
    earlier, recent = history_ref.shape[0], recent_ref.shape[0]
    snaps = earlier + recent
    chunk = math.gcd(modes, 16)
    group = math.gcd(rows, 8)

    def widen(i, _):
        block = modes_ref[pl.ds(i * chunk, chunk)].astype(jnp.float32)
        modes_wide[pl.ds(pl.multiple_of(i * chunk * rows, 8), chunk * rows), :] = block.reshape(
            chunk * rows, columns
        )
        return 0

    lax.fori_loop(0, modes // chunk, widen, 0)

    def widen_history(i, _):
        snaps_wide[pl.ds(pl.multiple_of(i * rows, 8), rows), :] = history_ref[i].astype(jnp.float32)
        return 0

    lax.fori_loop(0, earlier, widen_history, 0)
    for i in range(recent):
        snaps_wide[pl.ds((earlier + i) * rows, rows), :] = recent_ref[i].astype(jnp.float32)

    @pl.when(pl.program_id(0) == 0)
    def _():
        gram_ref[...] = jnp.zeros(gram_ref.shape, jnp.float32)
        projected_ref[...] = jnp.zeros(projected_ref.shape, jnp.float32)

    contract_last = (((1,), (1,)), ((), ()))

    def add(i, _):
        weighted, plain, shots = [], [], []
        masses = mass_ref[pl.ds(pl.multiple_of(i * group, group), group), :]
        for j in range(group):
            row = i * group + j
            shape = modes_wide[pl.ds(row, modes, stride=rows), :]
            weighted.append((shape * masses[j : j + 1, :]).astype(jnp.bfloat16))
            plain.append(shape.astype(jnp.bfloat16))
            shots.append(snaps_wide[pl.ds(row, snaps, stride=rows), :].astype(jnp.bfloat16))
        left = jnp.concatenate(weighted, axis=1)
        gram_ref[...] += lax.dot_general(
            left, jnp.concatenate(plain, axis=1), contract_last,
            preferred_element_type=jnp.float32,
        )
        projected_ref[...] += lax.dot_general(
            left, jnp.concatenate(shots, axis=1), contract_last,
            preferred_element_type=jnp.float32,
        )
        return 0

    lax.fori_loop(0, rows // group, add, 0)


def products(mode_shapes, mass, history, recent):
    modes, parts, rows, columns = mode_shapes.shape
    earlier, later = history.shape[0], recent.shape[0]
    snaps = earlier + later
    f32 = jnp.float32
    return pl.pallas_call(
        products_kernel,
        grid=(parts,),
        out_shape=(
            jax.ShapeDtypeStruct((modes, modes), f32),
            jax.ShapeDtypeStruct((modes, snaps), f32),
        ),
        in_specs=[
            pl.BlockSpec((modes, None, rows, columns), lambda c: (0, c, 0, 0)),
            pl.BlockSpec((rows, columns), lambda c: (0, 0)),
            pl.BlockSpec((earlier, None, rows, columns), lambda c: (0, c, 0, 0)),
            pl.BlockSpec((later, None, rows, columns), lambda c: (0, c, 0, 0)),
        ],
        out_specs=(
            pl.BlockSpec((modes, modes), lambda c: (0, 0)),
            pl.BlockSpec((modes, snaps), lambda c: (0, 0)),
        ),
        scratch_shapes=[
            pltpu.VMEM((modes * rows, columns), f32),
            pltpu.VMEM((snaps * rows, columns), f32),
        ],
        compiler_params=pltpu.CompilerParams(vmem_limit_bytes=vmem_limit),
        name="products",
    )(mode_shapes, mass, history, recent)


def body(
    displacement,
    velocity,
    lumped_mass,
    plastic_strain,
    hardening_strain,
    material_ids,
    material_table,
    ground_accel,
    snapshot_history,
    mode_shapes,
):
    disp_end, velo_end, plastic_end, harden_end, new_snaps = run_steps(
        displacement[:, 0], velocity[:, 0], lumped_mass[0], plastic_strain[:, :, 0],
        hardening_strain[:, :, 0], material_ids[:, :, 0], material_table, ground_accel,
    )
    mass_gram, projected = products(
        mode_shapes[:, :, 0], lumped_mass[0], snapshot_history[:, :, 0], new_snaps
    )
    gram = gram_total(mass_gram)
    modal_coords = coords_total(solve(gram, projected))
    return (
        disp_end[:, None], velo_end[:, None], plastic_end[:, :, None], harden_end[:, :, None],
        modal_coords,
    )


def solution(mesh):
    return jax.shard_map(
        body,
        mesh=mesh,
        in_specs=(
            P(None, "height", None, "plan"),
            P(None, "height", None, "plan"),
            P("height", None, "plan"),
            P(None, None, "height", None, "plan"),
            P(None, None, "height", None, "plan"),
            P(None, None, "height", None, "plan"),
            P(),
            P(),
            P(None, None, "height", None, "plan"),
            P(None, None, "height", None, "plan"),
        ),
        out_specs=(
            P(None, "height", None, "plan"),
            P(None, "height", None, "plan"),
            P(None, None, "height", None, "plan"),
            P(None, None, "height", None, "plan"),
            P(("height", "plan"), None),
        ),
        check_vma=False,
    )
```

```python
import functools
import math

import jax
import jax.numpy as jnp
from jax import lax
from jax.experimental import pallas as pl
from jax.experimental.pallas import tpu as pltpu
from jax.sharding import PartitionSpec as P

time_step = 0.3
mass_damping = 0.1
stiff_damping = 0.05
shear_stiff = 0.5
axial_components = (2, 1, 0)
HIGHEST = lax.Precision.HIGHEST
vmem_limit = 48 * 1024 * 1024


def mesh_id(linear, plan):
    return {"height": lax.div(linear, plan), "plan": lax.rem(linear, plan)}


def signal(semaphore, device):
    pl.semaphore_signal(semaphore, inc=1, device_id=device, device_id_type=pl.DeviceIdType.MESH)


def remote(source, target, send_sem, recv_sem, device):
    return pltpu.make_async_remote_copy(
        src_ref=source,
        dst_ref=target,
        send_sem=send_sem,
        recv_sem=recv_sem,
        device_id=device,
        device_id_type=pl.DeviceIdType.MESH,
    )


def greet_all(me, count, plan):
    barrier = pltpu.get_barrier_semaphore()

    def greet(offset, _):
        signal(barrier, mesh_id(lax.rem(me + offset, count), plan))
        return 0

    lax.fori_loop(1, count, greet, 0)
    return barrier


def wait_bytes(ref, semaphore):
    pltpu.make_async_copy(ref, ref, semaphore).wait()


def material_props(ids, table_ref):
    kinds = table_ref.shape[0]
    modulus = jnp.full(ids.shape, table_ref[0, 0], jnp.float32)
    yields = jnp.full(ids.shape, 0.4 * table_ref[0, 1], jnp.float32)
    slopes = jnp.full(ids.shape, 0.1 * table_ref[0, 2], jnp.float32)
    for kind in range(1, kinds):
        chosen = ids == kind
        modulus = jnp.where(chosen, table_ref[kind, 0], modulus)
        yields = jnp.where(chosen, 0.4 * table_ref[kind, 1], yields)
        slopes = jnp.where(chosen, 0.1 * table_ref[kind, 2], slopes)
    return modulus, yields, slopes, 1.0 / (modulus + slopes)


def fibre_step(stretch, plastic, harden, modulus, yields, slopes, inverse):
    trial = modulus * (stretch - plastic)
    excess = jnp.abs(trial) - (yields + slopes * harden)
    growth = jnp.maximum(excess, 0.0) * inverse
    signed = jnp.where(trial < 0.0, -growth, growth)
    return trial - modulus * signed, plastic + signed, harden + growth


def steps_kernel(
    heights, plan,
    disp_in, velo_in, mass_in, plastic_in, harden_in, ids_in, table_ref, accel_ref, part_ref,
    disp_out, velo_out, plastic_out, harden_out, snaps_out, gram_ref,
    velos, props, top_plastic, top_harden, top_ids, top_props,
    near_disp, near_velo, edge_send, edge_recv,
    disp_send_sem, disp_recv_sem, velo_send_sem, velo_recv_sem, state_send_sem, state_recv_sem,
    landed, total, part_send_sem, part_recv_sem, give_sem, take_sem,
):
    h, p = lax.axis_index("height"), lax.axis_index("plan")
    fibres = plastic_in.shape[1]
    rows, columns = mass_in.shape
    steps = accel_ref.shape[0]
    has_below, has_above = h > 0, h < heights - 1
    below = {"height": h - 1, "plan": p}
    above = {"height": h + 1, "plan": p}
    left = {"height": h, "plan": lax.rem(p + plan - 1, plan)}
    right = {"height": h, "plan": lax.rem(p + 1, plan)}
    lane = lax.broadcasted_iota(jnp.int32, (rows, columns), 1)
    row = lax.broadcasted_iota(jnp.int32, (rows, columns), 0)
    last = columns - 1

    count = heights * plan
    me = h * plan + p
    barrier = greet_all(me, count, plan)

    velos[0] = velo_in[...]
    packed = [jnp.zeros((rows, columns), jnp.float32) for _ in range(3)]
    for f in range(fibres):
        for part, value in enumerate(
            (plastic_in[2, f], harden_in[2, f], ids_in[2, f].astype(jnp.float32))
        ):
            packed[part] = jnp.where(lane == f, value[:, 0:1], packed[part])
    for part in range(3):
        edge_send[part] = packed[part]

    pl.semaphore_wait(barrier, count - 1)

    def disp_copy(side, device):
        return remote(
            disp_in, near_disp.at[side], disp_send_sem.at[side], disp_recv_sem.at[side], device
        )

    def velo_copy(side, step, device):
        return remote(
            velos.at[step], near_velo.at[step, side],
            velo_send_sem.at[step, side], velo_recv_sem.at[step, side], device,
        )

    def state_copies():
        return [
            remote(plastic_in.at[0], top_plastic, state_send_sem.at[0], state_recv_sem.at[0], below),
            remote(harden_in.at[0], top_harden, state_send_sem.at[1], state_recv_sem.at[1], below),
            remote(ids_in.at[0], top_ids, state_send_sem.at[2], state_recv_sem.at[2], below),
        ]

    edge_copy = remote(edge_send, edge_recv, state_send_sem.at[3], state_recv_sem.at[3], left)

    def exchange(step, first):
        copies = [lambda s, d: velo_copy(s, step, d)]
        if first:
            copies.append(disp_copy)

        @pl.when(has_above)
        def _():
            for make in copies:
                make(0, above).start()

        @pl.when(has_below)
        def _():
            for make in copies:
                make(1, below).start()

        for make in copies:
            make(2, right).start()
            make(3, left).start()

    def finish(step, first):
        copies = [lambda s, d: velo_copy(s, step, d)]
        if first:
            copies.append(disp_copy)

        @pl.when(has_below)
        def _():
            for make in copies:
                make(0, below).wait_recv()
                make(1, below).wait_send()

        @pl.when(has_above)
        def _():
            for make in copies:
                make(1, above).wait_recv()
                make(0, above).wait_send()

        for make in copies:
            for side, device in ((2, right), (3, left)):
                make(side, device).wait()

    exchange(0, True)
    edge_copy.start()

    @pl.when(has_below)
    def _():
        for copy in state_copies():
            copy.start()

    def send_part(offset, _):
        target = lax.rem(me + offset, count)
        remote(
            part_ref.at[target], landed.at[offset - 1], part_send_sem, part_recv_sem,
            mesh_id(target, plan),
        ).start()
        return 0

    lax.fori_loop(1, count, send_part, 0)

    def give_total(offset, _):
        target = lax.rem(me + offset, count)
        remote(total, gram_ref.at[me], give_sem, take_sem, mesh_id(target, plan)).start()
        return 0

    @pl.when(jnp.logical_not(has_below))
    def _():
        near_disp[0] = jnp.zeros(near_disp.shape[1:], jnp.float32)
        for step in range(steps):
            near_velo[step, 0] = jnp.zeros(near_velo.shape[2:], jnp.float32)

    @pl.when(jnp.logical_not(has_above))
    def _():
        near_disp[1] = jnp.zeros(near_disp.shape[1:], jnp.float32)
        for step in range(steps):
            near_velo[step, 1] = jnp.zeros(near_velo.shape[2:], jnp.float32)
        top_plastic[...] = jnp.zeros(top_plastic.shape, jnp.float32)
        top_harden[...] = jnp.zeros(top_harden.shape, jnp.float32)
        top_ids[...] = jnp.zeros(top_ids.shape, jnp.int32)

    zero = jnp.zeros((rows, columns), jnp.float32)

    def own_props(f, sums):
        new_sums = []
        for b in range(3):
            found = material_props(ids_in[b, f], table_ref)
            for part in range(4):
                props[part, b, f] = found[part]
            new_sums.append(sums[b] + found[0])
        return tuple(new_sums)

    sums = lax.fori_loop(0, fibres, own_props, (zero, zero, zero))
    tangents = [total * (1.0 / fibres) for total in sums]

    finish(0, True)
    edge_copy.wait()

    @pl.when(has_below)
    def _():
        for copy in state_copies():
            copy.wait_send()

    @pl.when(has_above)
    def _():
        for copy in state_copies():
            copy.wait_recv()

    def above_props(f, total):
        found = material_props(top_ids[f], table_ref)
        for part in range(4):
            top_props[part, f] = found[part]
        return total + found[0]

    top_tangent = lax.fori_loop(0, fibres, above_props, zero) * (1.0 / fibres)

    in_edge = lane < fibres
    edge_plastic, edge_harden = edge_recv[0], edge_recv[1]
    edge_found = material_props(edge_recv[2].astype(jnp.int32), table_ref)

    def edge_mean(value):
        return jnp.sum(jnp.where(in_edge, value, 0.0), axis=1, keepdims=True) * (1.0 / fibres)

    edge_tangent = edge_mean(edge_found[0])

    disp = [disp_in[c] for c in range(3)]
    velo = [velo_in[c] for c in range(3)]
    mass_inverse = 1.0 / mass_in[...]

    def rows_before(x):
        return jnp.where(row == 0, 0.0, pltpu.roll(x, 1, 0))

    def rows_after(x):
        return jnp.where(row == rows - 1, 0.0, pltpu.roll(x, rows - 1, 0))

    def rim_before(x, left_block):
        return pltpu.roll(jnp.where(lane == last, left_block, x), 1, 1)

    def shear(stretch, rate):
        return shear_stiff * (stretch + stiff_damping * rate)

    for step in range(steps):
        if step > 0:
            finish(step, False)
            for side in range(4):
                for c in range(3):
                    near_disp[side, c] = near_disp[side, c] + time_step * near_velo[step, side, c]
        source_plastic, source_harden = (
            (plastic_in, harden_in) if step == 0 else (plastic_out, harden_out)
        )
        stretch = [
            [disp[c] - near_disp[0, c] for c in range(3)],
            [disp[c] - rows_before(disp[c]) for c in range(3)],
            [disp[c] - rim_before(disp[c], near_disp[2, c]) for c in range(3)],
        ]
        rate = [
            [velo[c] - near_velo[step, 0, c] for c in range(3)],
            [velo[c] - rows_before(velo[c]) for c in range(3)],
            [velo[c] - rim_before(velo[c], near_velo[step, 2, c]) for c in range(3)],
        ]
        top_stretch = [near_disp[1, c] - disp[c] for c in range(3)]
        top_rate = [near_velo[step, 1, c] - velo[c] for c in range(3)]
        rim_stretch = [near_disp[3, c][:, 0:1] - disp[c][:, last:] for c in range(3)]
        rim_rate = [near_velo[step, 3, c][:, 0:1] - velo[c][:, last:] for c in range(3)]

        def fibre(f, totals):
            new_totals = []
            for b in range(3):
                stress, plastic, harden = fibre_step(
                    stretch[b][axial_components[b]], source_plastic[b, f], source_harden[b, f],
                    props[0, b, f], props[1, b, f], props[2, b, f], props[3, b, f],
                )
                plastic_out[b, f] = plastic
                harden_out[b, f] = harden
                new_totals.append(totals[b] + stress)
            stress, plastic, harden = fibre_step(
                top_stretch[axial_components[0]], top_plastic[f], top_harden[f],
                top_props[0, f], top_props[1, f], top_props[2, f], top_props[3, f],
            )
            top_plastic[f] = plastic
            top_harden[f] = harden
            new_totals.append(totals[3] + stress)
            return tuple(new_totals)

        totals = lax.fori_loop(0, fibres, fibre, (zero, zero, zero, zero))
        edge_stress, edge_plastic, edge_harden = fibre_step(
            rim_stretch[axial_components[2]], edge_plastic, edge_harden, *edge_found
        )
        edge_axial = edge_mean(edge_stress)

        new_velo = []
        for c in range(3):
            force = []
            for b in range(3):
                if c == axial_components[b]:
                    force.append(
                        totals[b] * (1.0 / fibres) + stiff_damping * tangents[b] * rate[b][c]
                    )
                else:
                    force.append(shear(stretch[b][c], rate[b][c]))
            if c == axial_components[0]:
                top = totals[3] * (1.0 / fibres) + stiff_damping * top_tangent * top_rate[c]
            else:
                top = shear(top_stretch[c], top_rate[c])
            if c == axial_components[2]:
                rim = edge_axial + stiff_damping * edge_tangent * rim_rate[c]
            else:
                rim = shear(rim_stretch[c], rim_rate[c])
            top = jnp.where(has_above, top, 0.0)
            after_rim = jnp.where(lane == last, rim, pltpu.roll(force[2], last, 1))
            resisting = (
                force[0] - top + (force[1] - rows_after(force[1])) + (force[2] - after_rim)
            )
            acceleration = -accel_ref[step, c] - resisting * mass_inverse
            new_velo.append(
                ((1.0 - 0.5 * mass_damping * time_step) * velo[c] + time_step * acceleration)
                * (1.0 / (1.0 + 0.5 * mass_damping * time_step))
            )
        velo = new_velo
        if step + 1 < steps:
            for c in range(3):
                velos[step + 1, c] = velo[c]
            exchange(step + 1, False)
        if step == 0:
            wait_bytes(landed, part_recv_sem)
            total[...] = part_ref[me] + jnp.sum(landed[...], axis=0)
            lax.fori_loop(1, count, give_total, 0)
            gram_ref[me] = total[...]
        for c in range(3):
            disp[c] = disp[c] + time_step * velo[c]
            snaps_out[step, c] = disp[c].astype(jnp.bfloat16)
    for c in range(3):
        disp_out[c] = disp[c]
        velo_out[c] = velo[c]
    wait_bytes(landed, take_sem)
    wait_bytes(landed, part_send_sem)
    wait_bytes(landed, give_sem)


def run_steps(disp, velo, mass, plastic, harden, ids, table, accel, part):
    heights, plan = lax.axis_size("height"), lax.axis_size("plan")
    steps = accel.shape[0]
    vmem = pl.BlockSpec(memory_space=pltpu.VMEM)
    smem = pl.BlockSpec(memory_space=pltpu.SMEM)
    f32 = jnp.float32
    fibres = plastic.shape[1]
    plane = mass.shape
    count = heights * plan
    modes = part.shape[0]
    blocks = (count, modes // count, modes)
    *ends, gram = pl.pallas_call(
        functools.partial(steps_kernel, heights, plan),
        out_shape=(
            jax.ShapeDtypeStruct(disp.shape, f32),
            jax.ShapeDtypeStruct(velo.shape, f32),
            jax.ShapeDtypeStruct(plastic.shape, f32),
            jax.ShapeDtypeStruct(harden.shape, f32),
            jax.ShapeDtypeStruct((steps,) + disp.shape, jnp.bfloat16),
            jax.ShapeDtypeStruct(blocks, f32),
        ),
        in_specs=[vmem] * 6 + [smem] * 2 + [vmem],
        out_specs=(vmem,) * 6,
        scratch_shapes=[
            pltpu.VMEM((steps,) + velo.shape, f32),
            pltpu.VMEM((4,) + plastic.shape, f32),
            pltpu.VMEM((fibres,) + plane, f32),
            pltpu.VMEM((fibres,) + plane, f32),
            pltpu.VMEM((fibres,) + plane, jnp.int32),
            pltpu.VMEM((4, fibres) + plane, f32),
            pltpu.VMEM((4,) + disp.shape, f32),
            pltpu.VMEM((steps, 4) + velo.shape, f32),
            pltpu.VMEM((3,) + plane, f32),
            pltpu.VMEM((3,) + plane, f32),
            pltpu.SemaphoreType.DMA((4,)),
            pltpu.SemaphoreType.DMA((4,)),
            pltpu.SemaphoreType.DMA((steps, 4)),
            pltpu.SemaphoreType.DMA((steps, 4)),
            pltpu.SemaphoreType.DMA((4,)),
            pltpu.SemaphoreType.DMA((4,)),
            pltpu.VMEM((count - 1,) + blocks[1:], f32),
            pltpu.VMEM(blocks[1:], f32),
        ]
        + [pltpu.SemaphoreType.DMA] * 4,
        compiler_params=pltpu.CompilerParams(
            collective_id=0, has_side_effects=True, vmem_limit_bytes=vmem_limit
        ),
        name="time_steps",
    )(disp, velo, mass, plastic, harden, ids, table, accel, part.reshape(blocks))
    return *ends, gram.reshape(modes, modes)


def coords_kernel(count, plan, part_ref, out_ref, landed, send_sem, recv_sem):
    me = lax.axis_index("height") * plan + lax.axis_index("plan")
    barrier = greet_all(me, count, plan)
    pl.semaphore_wait(barrier, count - 1)

    def send(offset, _):
        target = lax.rem(me + offset, count)
        remote(
            part_ref.at[target], landed.at[offset - 1], send_sem, recv_sem, mesh_id(target, plan)
        ).start()
        return 0

    lax.fori_loop(1, count, send, 0)
    wait_bytes(landed, recv_sem)
    out_ref[...] = part_ref[me] + jnp.sum(landed[...], axis=0)
    wait_bytes(landed, send_sem)


def coords_total(part):
    plan = lax.axis_size("plan")
    count = lax.axis_size(("height", "plan"))
    modes, snaps = part.shape
    rows = modes // count
    vmem = pl.BlockSpec(memory_space=pltpu.VMEM)
    return pl.pallas_call(
        functools.partial(coords_kernel, count, plan),
        out_shape=jax.ShapeDtypeStruct((rows, snaps), jnp.float32),
        in_specs=[vmem],
        out_specs=vmem,
        scratch_shapes=[pltpu.VMEM((count - 1, rows, snaps), jnp.float32)]
        + [pltpu.SemaphoreType.DMA] * 2,
        compiler_params=pltpu.CompilerParams(
            collective_id=2, has_side_effects=True, vmem_limit_bytes=vmem_limit
        ),
        name="coords_sum",
    )(part.reshape(count, rows, snaps))


def solve_kernel(gram_ref, projected_ref, out_ref):
    modes = gram_ref.shape[0]
    row = lax.broadcasted_iota(jnp.int32, (modes, modes), 0)
    column = lax.broadcasted_iota(jnp.int32, (modes, modes), 1)
    lower = jnp.where(row >= column, gram_ref[...], 0.0)
    gram = lower + jnp.where(row == column, 0.0, lower).T
    identity = jnp.where(row == column, 1.0, 0.0)
    size = jnp.max(jnp.sum(jnp.abs(gram), axis=1))
    guess = identity * (1.0 / size)

    def multiply(a, b):
        return jnp.dot(a, b, precision=HIGHEST, preferred_element_type=jnp.float32)

    def unfinished(state):
        turns, error, _ = state
        return jnp.logical_and(turns < 60, error > 1e-3)

    def improve(state):
        turns, _, inverse = state
        residual = identity - multiply(gram, inverse)
        error = jnp.max(jnp.sum(jnp.abs(residual), axis=0))
        return turns + 1, error, inverse + multiply(inverse, residual)

    _, _, inverse = lax.while_loop(unfinished, improve, (0, jnp.float32(2.0), guess))
    out_ref[...] = multiply(inverse, projected_ref[...])


def solve(gram, projected):
    vmem = pl.BlockSpec(memory_space=pltpu.VMEM)
    return pl.pallas_call(
        solve_kernel,
        out_shape=jax.ShapeDtypeStruct(projected.shape, jnp.float32),
        in_specs=[vmem, vmem],
        out_specs=vmem,
        compiler_params=pltpu.CompilerParams(vmem_limit_bytes=vmem_limit),
        name="solve",
    )(gram, projected)


def products_kernel(
    modes_ref, mass_ref, history_ref, gram_ref, projected_ref, weighted_ref, modes_wide, snaps_wide
):
    modes, rows, columns = modes_ref.shape
    earlier, snaps = history_ref.shape[0], projected_ref.shape[1]
    chunk = math.gcd(modes, 16)
    group = math.gcd(rows, 8)

    def widen(i, _):
        block = modes_ref[pl.ds(i * chunk, chunk)].astype(jnp.float32)
        modes_wide[pl.ds(pl.multiple_of(i * chunk * rows, 8), chunk * rows), :] = block.reshape(
            chunk * rows, columns
        )
        return 0

    lax.fori_loop(0, modes // chunk, widen, 0)

    def widen_history(i, _):
        snaps_wide[pl.ds(pl.multiple_of(i * rows, 8), rows), :] = history_ref[i].astype(jnp.float32)
        return 0

    lax.fori_loop(0, earlier, widen_history, 0)
    snaps_wide[earlier * rows :, :] = jnp.zeros(((snaps - earlier) * rows, columns), jnp.float32)

    @pl.when(pl.program_id(0) == 0)
    def _():
        gram_ref[...] = jnp.zeros(gram_ref.shape, jnp.float32)
        projected_ref[...] = jnp.zeros(projected_ref.shape, jnp.float32)

    contract_last = (((1,), (1,)), ((), ()))

    def add(i, _):
        weighted, plain, shots = [], [], []
        masses = mass_ref[pl.ds(pl.multiple_of(i * group, group), group), :]
        for j in range(group):
            row = i * group + j
            shape = modes_wide[pl.ds(row, modes, stride=rows), :]
            weighted.append((shape * masses[j : j + 1, :]).astype(jnp.bfloat16))
            plain.append(shape.astype(jnp.bfloat16))
            shots.append(snaps_wide[pl.ds(row, snaps, stride=rows), :].astype(jnp.bfloat16))
        left = jnp.concatenate(weighted, axis=1)
        weighted_ref[i] = left
        gram_ref[...] += lax.dot_general(
            left, jnp.concatenate(plain, axis=1), contract_last,
            preferred_element_type=jnp.float32,
        )
        projected_ref[...] += lax.dot_general(
            left, jnp.concatenate(shots, axis=1), contract_last,
            preferred_element_type=jnp.float32,
        )
        return 0

    lax.fori_loop(0, rows // group, add, 0)


def products(mode_shapes, mass, history, snaps):
    modes, parts, rows, columns = mode_shapes.shape
    earlier = history.shape[0]
    group = math.gcd(rows, 8)
    wide = (rows // group, modes, group * columns)
    f32 = jnp.float32
    return pl.pallas_call(
        products_kernel,
        grid=(parts,),
        out_shape=(
            jax.ShapeDtypeStruct((modes, modes), f32),
            jax.ShapeDtypeStruct((modes, snaps), f32),
            jax.ShapeDtypeStruct((parts,) + wide, jnp.bfloat16),
        ),
        in_specs=[
            pl.BlockSpec((modes, None, rows, columns), lambda c: (0, c, 0, 0)),
            pl.BlockSpec((rows, columns), lambda c: (0, 0)),
            pl.BlockSpec((earlier, None, rows, columns), lambda c: (0, c, 0, 0)),
        ],
        out_specs=(
            pl.BlockSpec((modes, modes), lambda c: (0, 0)),
            pl.BlockSpec((modes, snaps), lambda c: (0, 0)),
            pl.BlockSpec((None,) + wide, lambda c: (c, 0, 0, 0)),
        ),
        scratch_shapes=[
            pltpu.VMEM((modes * rows, columns), f32),
            pltpu.VMEM((snaps * rows, columns), f32),
        ],
        compiler_params=pltpu.CompilerParams(vmem_limit_bytes=vmem_limit),
        name="products",
    )(mode_shapes, mass, history)


def recent_kernel(weighted_ref, recent_ref, before_ref, projected_ref, snaps_wide):
    groups, modes, depth = weighted_ref.shape
    recent, rows, columns = recent_ref.shape
    snaps = projected_ref.shape[1]
    earlier = snaps - recent
    group = rows // groups

    @pl.when(pl.program_id(0) == 0)
    def _():
        snaps_wide[: earlier * rows, :] = jnp.zeros((earlier * rows, columns), jnp.float32)
        projected_ref[...] = before_ref[...]

    for i in range(recent):
        snaps_wide[pl.ds((earlier + i) * rows, rows), :] = recent_ref[i].astype(jnp.float32)
    for i in range(groups):
        shots = [
            snaps_wide[pl.ds(i * group + j, snaps, stride=rows), :].astype(jnp.bfloat16)
            for j in range(group)
        ]
        projected_ref[...] += lax.dot_general(
            weighted_ref[i], jnp.concatenate(shots, axis=1), (((1,), (1,)), ((), ())),
            preferred_element_type=jnp.float32,
        )


def add_recent(weighted, recent, before):
    parts, groups, modes, depth = weighted.shape
    later, _, rows, columns = recent.shape
    snaps = before.shape[1]
    return pl.pallas_call(
        recent_kernel,
        grid=(parts,),
        out_shape=jax.ShapeDtypeStruct(before.shape, jnp.float32),
        in_specs=[
            pl.BlockSpec((None, groups, modes, depth), lambda c: (c, 0, 0, 0)),
            pl.BlockSpec((later, None, rows, columns), lambda c: (0, c, 0, 0)),
            pl.BlockSpec((modes, snaps), lambda c: (0, 0)),
        ],
        out_specs=pl.BlockSpec((modes, snaps), lambda c: (0, 0)),
        scratch_shapes=[pltpu.VMEM((snaps * rows, columns), jnp.float32)],
        compiler_params=pltpu.CompilerParams(vmem_limit_bytes=vmem_limit),
        name="recent_products",
    )(weighted, recent, before)


def body(
    displacement,
    velocity,
    lumped_mass,
    plastic_strain,
    hardening_strain,
    material_ids,
    material_table,
    ground_accel,
    snapshot_history,
    mode_shapes,
):
    snaps = snapshot_history.shape[0] + ground_accel.shape[0]
    mass_gram, projected, weighted = products(
        mode_shapes[:, :, 0], lumped_mass[0], snapshot_history[:, :, 0], snaps
    )
    disp_end, velo_end, plastic_end, harden_end, new_snaps, gram = run_steps(
        displacement[:, 0], velocity[:, 0], lumped_mass[0], plastic_strain[:, :, 0],
        hardening_strain[:, :, 0], material_ids[:, :, 0], material_table, ground_accel, mass_gram,
    )
    projected = add_recent(weighted, new_snaps, projected)
    modal_coords = coords_total(solve(gram, projected))
    return (
        disp_end[:, None], velo_end[:, None], plastic_end[:, :, None], harden_end[:, :, None],
        modal_coords,
    )


def solution(mesh):
    return jax.shard_map(
        body,
        mesh=mesh,
        in_specs=(
            P(None, "height", None, "plan"),
            P(None, "height", None, "plan"),
            P("height", None, "plan"),
            P(None, None, "height", None, "plan"),
            P(None, None, "height", None, "plan"),
            P(None, None, "height", None, "plan"),
            P(),
            P(),
            P(None, None, "height", None, "plan"),
            P(None, None, "height", None, "plan"),
        ),
        out_specs=(
            P(None, "height", None, "plan"),
            P(None, "height", None, "plan"),
            P(None, None, "height", None, "plan"),
            P(None, None, "height", None, "plan"),
            P(("height", "plan"), None),
        ),
        check_vma=False,
    )
```

```python
import functools
import math

import jax
import jax.numpy as jnp
from jax import lax
from jax.experimental import pallas as pl
from jax.experimental.pallas import tpu as pltpu
from jax.sharding import PartitionSpec as P

time_step = 0.3
mass_damping = 0.1
stiff_damping = 0.05
shear_stiff = 0.5
axial_components = (2, 1, 0)
HIGHEST = lax.Precision.HIGHEST
vmem_limit = 48 * 1024 * 1024


def mesh_id(linear, plan):
    return {"height": lax.div(linear, plan), "plan": lax.rem(linear, plan)}


def signal(semaphore, device):
    pl.semaphore_signal(semaphore, inc=1, device_id=device, device_id_type=pl.DeviceIdType.MESH)


def remote(source, target, send_sem, recv_sem, device):
    return pltpu.make_async_remote_copy(
        src_ref=source,
        dst_ref=target,
        send_sem=send_sem,
        recv_sem=recv_sem,
        device_id=device,
        device_id_type=pl.DeviceIdType.MESH,
    )


def greet_all(me, count, plan):
    barrier = pltpu.get_barrier_semaphore()

    def greet(offset, _):
        signal(barrier, mesh_id(lax.rem(me + offset, count), plan))
        return 0

    lax.fori_loop(1, count, greet, 0)
    return barrier


def wait_bytes(ref, semaphore):
    pltpu.make_async_copy(ref, ref, semaphore).wait()


def material_props(ids, table_ref):
    kinds = table_ref.shape[0]
    modulus = jnp.full(ids.shape, table_ref[0, 0], jnp.float32)
    yields = jnp.full(ids.shape, 0.4 * table_ref[0, 1], jnp.float32)
    slopes = jnp.full(ids.shape, 0.1 * table_ref[0, 2], jnp.float32)
    for kind in range(1, kinds):
        chosen = ids == kind
        modulus = jnp.where(chosen, table_ref[kind, 0], modulus)
        yields = jnp.where(chosen, 0.4 * table_ref[kind, 1], yields)
        slopes = jnp.where(chosen, 0.1 * table_ref[kind, 2], slopes)
    return modulus, yields, slopes, 1.0 / (modulus + slopes)


def fibre_step(stretch, plastic, harden, modulus, yields, slopes, inverse):
    trial = modulus * (stretch - plastic)
    excess = jnp.abs(trial) - (yields + slopes * harden)
    growth = jnp.maximum(excess, 0.0) * inverse
    signed = jnp.where(trial < 0.0, -growth, growth)
    return trial - modulus * signed, plastic + signed, harden + growth


def steps_kernel(
    heights, plan,
    disp_in, velo_in, mass_in, plastic_in, harden_in, ids_in, table_ref, accel_ref, part_ref,
    disp_out, velo_out, plastic_out, harden_out, snaps_out, gram_ref,
    velos, props, top_plastic, top_harden, top_ids, top_props,
    near_disp, near_velo, edge_send, edge_recv,
    disp_send_sem, disp_recv_sem, velo_send_sem, velo_recv_sem, state_send_sem, state_recv_sem,
    landed, total, part_send_sem, part_recv_sem, give_sem, take_sem,
):
    h, p = lax.axis_index("height"), lax.axis_index("plan")
    fibres = plastic_in.shape[1]
    rows, columns = mass_in.shape
    steps = accel_ref.shape[0]
    has_below, has_above = h > 0, h < heights - 1
    below = {"height": h - 1, "plan": p}
    above = {"height": h + 1, "plan": p}
    left = {"height": h, "plan": lax.rem(p + plan - 1, plan)}
    right = {"height": h, "plan": lax.rem(p + 1, plan)}
    lane = lax.broadcasted_iota(jnp.int32, (rows, columns), 1)
    row = lax.broadcasted_iota(jnp.int32, (rows, columns), 0)
    last = columns - 1

    count = heights * plan
    me = h * plan + p
    barrier = greet_all(me, count, plan)

    velos[0] = velo_in[...]
    packed = [jnp.zeros((rows, columns), jnp.float32) for _ in range(3)]
    for f in range(fibres):
        for part, value in enumerate(
            (plastic_in[2, f], harden_in[2, f], ids_in[2, f].astype(jnp.float32))
        ):
            packed[part] = jnp.where(lane == f, value[:, 0:1], packed[part])
    for part in range(3):
        edge_send[part] = packed[part]

    pl.semaphore_wait(barrier, count - 1)

    def disp_copy(side, device):
        return remote(
            disp_in, near_disp.at[side], disp_send_sem.at[side], disp_recv_sem.at[side], device
        )

    def velo_copy(side, step, device):
        return remote(
            velos.at[step], near_velo.at[step, side],
            velo_send_sem.at[step, side], velo_recv_sem.at[step, side], device,
        )

    def state_copies():
        return [
            remote(plastic_in.at[0], top_plastic, state_send_sem.at[0], state_recv_sem.at[0], below),
            remote(harden_in.at[0], top_harden, state_send_sem.at[1], state_recv_sem.at[1], below),
            remote(ids_in.at[0], top_ids, state_send_sem.at[2], state_recv_sem.at[2], below),
        ]

    edge_copy = remote(edge_send, edge_recv, state_send_sem.at[3], state_recv_sem.at[3], left)

    def exchange(step, first):
        copies = [lambda s, d: velo_copy(s, step, d)]
        if first:
            copies.append(disp_copy)

        @pl.when(has_above)
        def _():
            for make in copies:
                make(0, above).start()

        @pl.when(has_below)
        def _():
            for make in copies:
                make(1, below).start()

        for make in copies:
            make(2, right).start()
            make(3, left).start()

    def finish(step, first):
        copies = [lambda s, d: velo_copy(s, step, d)]
        if first:
            copies.append(disp_copy)

        @pl.when(has_below)
        def _():
            for make in copies:
                make(0, below).wait_recv()
                make(1, below).wait_send()

        @pl.when(has_above)
        def _():
            for make in copies:
                make(1, above).wait_recv()
                make(0, above).wait_send()

        for make in copies:
            for side, device in ((2, right), (3, left)):
                make(side, device).wait()

    exchange(0, True)
    edge_copy.start()

    @pl.when(has_below)
    def _():
        for copy in state_copies():
            copy.start()

    def send_part(offset, _):
        target = lax.rem(me + offset, count)
        remote(
            part_ref.at[target], landed.at[offset - 1], part_send_sem, part_recv_sem,
            mesh_id(target, plan),
        ).start()
        return 0

    lax.fori_loop(1, count, send_part, 0)

    def give_total(offset, _):
        target = lax.rem(me + offset, count)
        remote(total, gram_ref.at[me], give_sem, take_sem, mesh_id(target, plan)).start()
        return 0

    @pl.when(jnp.logical_not(has_below))
    def _():
        near_disp[0] = jnp.zeros(near_disp.shape[1:], jnp.float32)
        for step in range(steps):
            near_velo[step, 0] = jnp.zeros(near_velo.shape[2:], jnp.float32)

    @pl.when(jnp.logical_not(has_above))
    def _():
        near_disp[1] = jnp.zeros(near_disp.shape[1:], jnp.float32)
        for step in range(steps):
            near_velo[step, 1] = jnp.zeros(near_velo.shape[2:], jnp.float32)
        top_plastic[...] = jnp.zeros(top_plastic.shape, jnp.float32)
        top_harden[...] = jnp.zeros(top_harden.shape, jnp.float32)
        top_ids[...] = jnp.zeros(top_ids.shape, jnp.int32)

    zero = jnp.zeros((rows, columns), jnp.float32)

    def own_props(f, sums):
        new_sums = []
        for b in range(3):
            found = material_props(ids_in[b, f], table_ref)
            for part in range(4):
                props[part, b, f] = found[part]
            new_sums.append(sums[b] + found[0])
        return tuple(new_sums)

    sums = lax.fori_loop(0, fibres, own_props, (zero, zero, zero))
    tangents = [total * (1.0 / fibres) for total in sums]

    finish(0, True)
    edge_copy.wait()

    @pl.when(has_below)
    def _():
        for copy in state_copies():
            copy.wait_send()

    @pl.when(has_above)
    def _():
        for copy in state_copies():
            copy.wait_recv()

    def above_props(f, total):
        found = material_props(top_ids[f], table_ref)
        for part in range(4):
            top_props[part, f] = found[part]
        return total + found[0]

    top_tangent = lax.fori_loop(0, fibres, above_props, zero) * (1.0 / fibres)

    in_edge = lane < fibres
    edge_plastic, edge_harden = edge_recv[0], edge_recv[1]
    edge_found = material_props(edge_recv[2].astype(jnp.int32), table_ref)

    def edge_mean(value):
        return jnp.sum(jnp.where(in_edge, value, 0.0), axis=1, keepdims=True) * (1.0 / fibres)

    edge_tangent = edge_mean(edge_found[0])

    disp = [disp_in[c] for c in range(3)]
    velo = [velo_in[c] for c in range(3)]
    mass_inverse = 1.0 / mass_in[...]

    def rows_before(x):
        return jnp.where(row == 0, 0.0, pltpu.roll(x, 1, 0))

    def rows_after(x):
        return jnp.where(row == rows - 1, 0.0, pltpu.roll(x, rows - 1, 0))

    def rim_before(x, left_block):
        return pltpu.roll(jnp.where(lane == last, left_block, x), 1, 1)

    def shear(stretch, rate):
        return shear_stiff * (stretch + stiff_damping * rate)

    for step in range(steps):
        if step > 0:
            finish(step, False)
            for side in range(4):
                for c in range(3):
                    near_disp[side, c] = near_disp[side, c] + time_step * near_velo[step, side, c]
        source_plastic, source_harden = (
            (plastic_in, harden_in) if step == 0 else (plastic_out, harden_out)
        )
        stretch = [
            [disp[c] - near_disp[0, c] for c in range(3)],
            [disp[c] - rows_before(disp[c]) for c in range(3)],
            [disp[c] - rim_before(disp[c], near_disp[2, c]) for c in range(3)],
        ]
        rate = [
            [velo[c] - near_velo[step, 0, c] for c in range(3)],
            [velo[c] - rows_before(velo[c]) for c in range(3)],
            [velo[c] - rim_before(velo[c], near_velo[step, 2, c]) for c in range(3)],
        ]
        top_stretch = [near_disp[1, c] - disp[c] for c in range(3)]
        top_rate = [near_velo[step, 1, c] - velo[c] for c in range(3)]
        rim_stretch = [near_disp[3, c][:, 0:1] - disp[c][:, last:] for c in range(3)]
        rim_rate = [near_velo[step, 3, c][:, 0:1] - velo[c][:, last:] for c in range(3)]

        def fibre(f, totals):
            new_totals = []
            for b in range(3):
                stress, plastic, harden = fibre_step(
                    stretch[b][axial_components[b]], source_plastic[b, f], source_harden[b, f],
                    props[0, b, f], props[1, b, f], props[2, b, f], props[3, b, f],
                )
                plastic_out[b, f] = plastic
                harden_out[b, f] = harden
                new_totals.append(totals[b] + stress)
            stress, plastic, harden = fibre_step(
                top_stretch[axial_components[0]], top_plastic[f], top_harden[f],
                top_props[0, f], top_props[1, f], top_props[2, f], top_props[3, f],
            )
            top_plastic[f] = plastic
            top_harden[f] = harden
            new_totals.append(totals[3] + stress)
            return tuple(new_totals)

        totals = lax.fori_loop(0, fibres, fibre, (zero, zero, zero, zero))
        edge_stress, edge_plastic, edge_harden = fibre_step(
            rim_stretch[axial_components[2]], edge_plastic, edge_harden, *edge_found
        )
        edge_axial = edge_mean(edge_stress)

        new_velo = []
        for c in range(3):
            force = []
            for b in range(3):
                if c == axial_components[b]:
                    force.append(
                        totals[b] * (1.0 / fibres) + stiff_damping * tangents[b] * rate[b][c]
                    )
                else:
                    force.append(shear(stretch[b][c], rate[b][c]))
            if c == axial_components[0]:
                top = totals[3] * (1.0 / fibres) + stiff_damping * top_tangent * top_rate[c]
            else:
                top = shear(top_stretch[c], top_rate[c])
            if c == axial_components[2]:
                rim = edge_axial + stiff_damping * edge_tangent * rim_rate[c]
            else:
                rim = shear(rim_stretch[c], rim_rate[c])
            top = jnp.where(has_above, top, 0.0)
            after_rim = jnp.where(lane == last, rim, pltpu.roll(force[2], last, 1))
            resisting = (
                force[0] - top + (force[1] - rows_after(force[1])) + (force[2] - after_rim)
            )
            acceleration = -accel_ref[step, c] - resisting * mass_inverse
            new_velo.append(
                ((1.0 - 0.5 * mass_damping * time_step) * velo[c] + time_step * acceleration)
                * (1.0 / (1.0 + 0.5 * mass_damping * time_step))
            )
        velo = new_velo
        if step + 1 < steps:
            for c in range(3):
                velos[step + 1, c] = velo[c]
            exchange(step + 1, False)
        if step == 0:
            wait_bytes(landed, part_recv_sem)
            total[...] = part_ref[me] + jnp.sum(landed[...], axis=0)
            lax.fori_loop(1, count, give_total, 0)
            gram_ref[me] = total[...]
        for c in range(3):
            disp[c] = disp[c] + time_step * velo[c]
            snaps_out[step, c] = disp[c].astype(jnp.bfloat16)
    for c in range(3):
        disp_out[c] = disp[c]
        velo_out[c] = velo[c]
    wait_bytes(landed, take_sem)
    wait_bytes(landed, part_send_sem)
    wait_bytes(landed, give_sem)


def run_steps(disp, velo, mass, plastic, harden, ids, table, accel, part):
    heights, plan = lax.axis_size("height"), lax.axis_size("plan")
    steps = accel.shape[0]
    vmem = pl.BlockSpec(memory_space=pltpu.VMEM)
    smem = pl.BlockSpec(memory_space=pltpu.SMEM)
    f32 = jnp.float32
    fibres = plastic.shape[1]
    plane = mass.shape
    count = heights * plan
    modes = part.shape[0]
    blocks = (count, modes // count, modes)
    *ends, gram = pl.pallas_call(
        functools.partial(steps_kernel, heights, plan),
        out_shape=(
            jax.ShapeDtypeStruct(disp.shape, f32),
            jax.ShapeDtypeStruct(velo.shape, f32),
            jax.ShapeDtypeStruct(plastic.shape, f32),
            jax.ShapeDtypeStruct(harden.shape, f32),
            jax.ShapeDtypeStruct((steps,) + disp.shape, jnp.bfloat16),
            jax.ShapeDtypeStruct(blocks, f32),
        ),
        in_specs=[vmem] * 6 + [smem] * 2 + [vmem],
        out_specs=(vmem,) * 6,
        scratch_shapes=[
            pltpu.VMEM((steps,) + velo.shape, f32),
            pltpu.VMEM((4,) + plastic.shape, f32),
            pltpu.VMEM((fibres,) + plane, f32),
            pltpu.VMEM((fibres,) + plane, f32),
            pltpu.VMEM((fibres,) + plane, jnp.int32),
            pltpu.VMEM((4, fibres) + plane, f32),
            pltpu.VMEM((4,) + disp.shape, f32),
            pltpu.VMEM((steps, 4) + velo.shape, f32),
            pltpu.VMEM((3,) + plane, f32),
            pltpu.VMEM((3,) + plane, f32),
            pltpu.SemaphoreType.DMA((4,)),
            pltpu.SemaphoreType.DMA((4,)),
            pltpu.SemaphoreType.DMA((steps, 4)),
            pltpu.SemaphoreType.DMA((steps, 4)),
            pltpu.SemaphoreType.DMA((4,)),
            pltpu.SemaphoreType.DMA((4,)),
            pltpu.VMEM((count - 1,) + blocks[1:], f32),
            pltpu.VMEM(blocks[1:], f32),
        ]
        + [pltpu.SemaphoreType.DMA] * 4,
        compiler_params=pltpu.CompilerParams(
            collective_id=0, has_side_effects=True, vmem_limit_bytes=vmem_limit
        ),
        name="time_steps",
    )(disp, velo, mass, plastic, harden, ids, table, accel, part.reshape(blocks))
    return *ends, gram.reshape(modes, modes)


def coords_kernel(count, plan, part_ref, out_ref, landed, send_sem, recv_sem):
    me = lax.axis_index("height") * plan + lax.axis_index("plan")
    barrier = greet_all(me, count, plan)
    pl.semaphore_wait(barrier, count - 1)

    def send(offset, _):
        target = lax.rem(me + offset, count)
        remote(
            part_ref.at[target], landed.at[offset - 1], send_sem, recv_sem, mesh_id(target, plan)
        ).start()
        return 0

    lax.fori_loop(1, count, send, 0)
    wait_bytes(landed, recv_sem)
    out_ref[...] = part_ref[me] + jnp.sum(landed[...], axis=0)
    wait_bytes(landed, send_sem)


def coords_total(part):
    plan = lax.axis_size("plan")
    count = lax.axis_size(("height", "plan"))
    modes, snaps = part.shape
    rows = modes // count
    vmem = pl.BlockSpec(memory_space=pltpu.VMEM)
    return pl.pallas_call(
        functools.partial(coords_kernel, count, plan),
        out_shape=jax.ShapeDtypeStruct((rows, snaps), jnp.float32),
        in_specs=[vmem],
        out_specs=vmem,
        scratch_shapes=[pltpu.VMEM((count - 1, rows, snaps), jnp.float32)]
        + [pltpu.SemaphoreType.DMA] * 2,
        compiler_params=pltpu.CompilerParams(
            collective_id=2, has_side_effects=True, vmem_limit_bytes=vmem_limit
        ),
        name="coords_sum",
    )(part.reshape(count, rows, snaps))


def solve_kernel(gram_ref, projected_ref, *refs):
    kept = (len(refs) - 2) // 2
    held, out_ref, handed, sems = refs[:kept], refs[kept], refs[kept + 1 : -1], refs[-1]
    copies = [
        pltpu.make_async_copy(source, target, sems.at[i])
        for i, (source, target) in enumerate(zip(held, handed))
    ]
    for copy in copies:
        copy.start()
    modes = gram_ref.shape[0]
    row = lax.broadcasted_iota(jnp.int32, (modes, modes), 0)
    column = lax.broadcasted_iota(jnp.int32, (modes, modes), 1)
    lower = jnp.where(row >= column, gram_ref[...], 0.0)
    gram = lower + jnp.where(row == column, 0.0, lower).T
    identity = jnp.where(row == column, 1.0, 0.0)
    size = jnp.max(jnp.sum(jnp.abs(gram), axis=0))
    guess = identity * (1.0 / size)
    rough_gram = gram.astype(jnp.bfloat16)

    def multiply(a, b):
        return jnp.dot(a, b, precision=HIGHEST, preferred_element_type=jnp.float32)

    def rough_multiply(a, b):
        return jnp.dot(a, b, preferred_element_type=jnp.float32)

    def length(residual):
        return jnp.max(jnp.sum(jnp.abs(residual), axis=0))

    def rough_unfinished(state):
        turns, error, _ = state
        return jnp.logical_and(turns < 12, error > 0.1)

    def rough_improve(state):
        turns, _, inverse = state
        narrow = inverse.astype(jnp.bfloat16)
        residual = identity - rough_multiply(rough_gram, narrow)
        step = rough_multiply(narrow, residual.astype(jnp.bfloat16))
        return turns + 1, length(residual), inverse + step

    _, _, start = lax.while_loop(rough_unfinished, rough_improve, (0, jnp.float32(2.0), guess))
    residual = identity - multiply(gram, start)
    usable = length(residual) < 0.9
    start = jnp.where(usable, start, guess)
    residual = jnp.where(usable, residual, identity - gram * (1.0 / size))

    def unfinished(state):
        turns, error, _, _ = state
        return jnp.logical_and(turns < 60, error > 3e-3)

    def improve(state):
        turns, _, inverse, residual = state
        inverse = inverse + multiply(inverse, residual)
        residual = identity - multiply(gram, inverse)
        return turns + 1, length(residual), inverse, residual

    _, _, inverse, residual = lax.while_loop(
        unfinished, improve, (0, length(residual), start, residual)
    )
    projected = projected_ref[...]
    out_ref[...] = multiply(inverse, projected + multiply(residual, projected))
    for copy in copies:
        copy.wait()


def solve(gram, projected, held):
    vmem = pl.BlockSpec(memory_space=pltpu.VMEM)
    anywhere = pl.BlockSpec(memory_space=pl.ANY)
    return pl.pallas_call(
        solve_kernel,
        out_shape=(jax.ShapeDtypeStruct(projected.shape, jnp.float32),)
        + tuple(jax.ShapeDtypeStruct(x.shape, x.dtype) for x in held),
        in_specs=[vmem, vmem] + [anywhere] * len(held),
        out_specs=(vmem,) + (anywhere,) * len(held),
        scratch_shapes=[pltpu.SemaphoreType.DMA((len(held),))],
        compiler_params=pltpu.CompilerParams(vmem_limit_bytes=vmem_limit),
        name="solve",
    )(gram, projected, *held)


def products_kernel(
    modes_ref, mass_ref, history_ref, gram_ref, projected_ref, weighted_ref, modes_wide, snaps_wide
):
    modes, rows, columns = modes_ref.shape
    earlier, snaps = history_ref.shape[0], projected_ref.shape[1]
    chunk = math.gcd(modes, 16)
    group = math.gcd(rows, 8)

    def widen(i, _):
        block = modes_ref[pl.ds(i * chunk, chunk)].astype(jnp.float32)
        modes_wide[pl.ds(pl.multiple_of(i * chunk * rows, 8), chunk * rows), :] = block.reshape(
            chunk * rows, columns
        )
        return 0

    lax.fori_loop(0, modes // chunk, widen, 0)

    def widen_history(i, _):
        snaps_wide[pl.ds(pl.multiple_of(i * rows, 8), rows), :] = history_ref[i].astype(jnp.float32)
        return 0

    lax.fori_loop(0, earlier, widen_history, 0)
    snaps_wide[earlier * rows :, :] = jnp.zeros(((snaps - earlier) * rows, columns), jnp.float32)

    @pl.when(pl.program_id(0) == 0)
    def _():
        gram_ref[...] = jnp.zeros(gram_ref.shape, jnp.float32)
        projected_ref[...] = jnp.zeros(projected_ref.shape, jnp.float32)

    contract_last = (((1,), (1,)), ((), ()))

    def add(i, _):
        weighted, plain, shots = [], [], []
        masses = mass_ref[pl.ds(pl.multiple_of(i * group, group), group), :]
        for j in range(group):
            row = i * group + j
            shape = modes_wide[pl.ds(row, modes, stride=rows), :]
            weighted.append((shape * masses[j : j + 1, :]).astype(jnp.bfloat16))
            plain.append(shape.astype(jnp.bfloat16))
            shots.append(snaps_wide[pl.ds(row, snaps, stride=rows), :].astype(jnp.bfloat16))
        left = jnp.concatenate(weighted, axis=1)
        weighted_ref[i] = left
        gram_ref[...] += lax.dot_general(
            left, jnp.concatenate(plain, axis=1), contract_last,
            preferred_element_type=jnp.float32,
        )
        projected_ref[...] += lax.dot_general(
            left, jnp.concatenate(shots, axis=1), contract_last,
            preferred_element_type=jnp.float32,
        )
        return 0

    lax.fori_loop(0, rows // group, add, 0)


def products(mode_shapes, mass, history, snaps):
    modes, parts, rows, columns = mode_shapes.shape
    earlier = history.shape[0]
    group = math.gcd(rows, 8)
    wide = (rows // group, modes, group * columns)
    f32 = jnp.float32
    return pl.pallas_call(
        products_kernel,
        grid=(parts,),
        out_shape=(
            jax.ShapeDtypeStruct((modes, modes), f32),
            jax.ShapeDtypeStruct((modes, snaps), f32),
            jax.ShapeDtypeStruct((parts,) + wide, jnp.bfloat16),
        ),
        in_specs=[
            pl.BlockSpec((modes, None, rows, columns), lambda c: (0, c, 0, 0)),
            pl.BlockSpec((rows, columns), lambda c: (0, 0)),
            pl.BlockSpec((earlier, None, rows, columns), lambda c: (0, c, 0, 0)),
        ],
        out_specs=(
            pl.BlockSpec((modes, modes), lambda c: (0, 0)),
            pl.BlockSpec((modes, snaps), lambda c: (0, 0)),
            pl.BlockSpec((None,) + wide, lambda c: (c, 0, 0, 0)),
        ),
        scratch_shapes=[
            pltpu.VMEM((modes * rows, columns), f32),
            pltpu.VMEM((snaps * rows, columns), f32),
        ],
        compiler_params=pltpu.CompilerParams(vmem_limit_bytes=vmem_limit),
        name="products",
    )(mode_shapes, mass, history)


def recent_kernel(weighted_ref, recent_ref, before_ref, projected_ref, snaps_wide):
    groups, modes, depth = weighted_ref.shape
    recent, rows, columns = recent_ref.shape
    snaps = projected_ref.shape[1]
    earlier = snaps - recent
    group = rows // groups

    @pl.when(pl.program_id(0) == 0)
    def _():
        snaps_wide[: earlier * rows, :] = jnp.zeros((earlier * rows, columns), jnp.float32)
        projected_ref[...] = before_ref[...]

    for i in range(recent):
        snaps_wide[pl.ds((earlier + i) * rows, rows), :] = recent_ref[i].astype(jnp.float32)
    for i in range(groups):
        shots = [
            snaps_wide[pl.ds(i * group + j, snaps, stride=rows), :].astype(jnp.bfloat16)
            for j in range(group)
        ]
        projected_ref[...] += lax.dot_general(
            weighted_ref[i], jnp.concatenate(shots, axis=1), (((1,), (1,)), ((), ())),
            preferred_element_type=jnp.float32,
        )


def add_recent(weighted, recent, before):
    parts, groups, modes, depth = weighted.shape
    later, _, rows, columns = recent.shape
    snaps = before.shape[1]
    return pl.pallas_call(
        recent_kernel,
        grid=(parts,),
        out_shape=jax.ShapeDtypeStruct(before.shape, jnp.float32),
        in_specs=[
            pl.BlockSpec((None, groups, modes, depth), lambda c: (c, 0, 0, 0)),
            pl.BlockSpec((later, None, rows, columns), lambda c: (0, c, 0, 0)),
            pl.BlockSpec((modes, snaps), lambda c: (0, 0)),
        ],
        out_specs=pl.BlockSpec((modes, snaps), lambda c: (0, 0)),
        scratch_shapes=[pltpu.VMEM((snaps * rows, columns), jnp.float32)],
        compiler_params=pltpu.CompilerParams(vmem_limit_bytes=vmem_limit),
        name="recent_products",
    )(weighted, recent, before)


def body(
    displacement,
    velocity,
    lumped_mass,
    plastic_strain,
    hardening_strain,
    material_ids,
    material_table,
    ground_accel,
    snapshot_history,
    mode_shapes,
):
    snaps = snapshot_history.shape[0] + ground_accel.shape[0]
    mass_gram, projected, weighted = products(
        mode_shapes[:, :, 0], lumped_mass[0], snapshot_history[:, :, 0], snaps
    )
    disp_end, velo_end, plastic_end, harden_end, new_snaps, gram = run_steps(
        displacement[:, 0], velocity[:, 0], lumped_mass[0], plastic_strain[:, :, 0],
        hardening_strain[:, :, 0], material_ids[:, :, 0], material_table, ground_accel, mass_gram,
    )
    projected = add_recent(weighted, new_snaps, projected)
    coords, disp_end, velo_end, plastic_end, harden_end = solve(
        gram, projected, (disp_end, velo_end, plastic_end, harden_end)
    )
    modal_coords = coords_total(coords)
    return (
        disp_end[:, None], velo_end[:, None], plastic_end[:, :, None], harden_end[:, :, None],
        modal_coords,
    )


def solution(mesh):
    return jax.shard_map(
        body,
        mesh=mesh,
        in_specs=(
            P(None, "height", None, "plan"),
            P(None, "height", None, "plan"),
            P("height", None, "plan"),
            P(None, None, "height", None, "plan"),
            P(None, None, "height", None, "plan"),
            P(None, None, "height", None, "plan"),
            P(),
            P(),
            P(None, None, "height", None, "plan"),
            P(None, None, "height", None, "plan"),
        ),
        out_specs=(
            P(None, "height", None, "plan"),
            P(None, "height", None, "plan"),
            P(None, None, "height", None, "plan"),
            P(None, None, "height", None, "plan"),
            P(("height", "plan"), None),
        ),
        check_vma=False,
    )
```

```python
import functools
import math

import jax
import jax.numpy as jnp
from jax import lax
from jax.experimental import pallas as pl
from jax.experimental.pallas import tpu as pltpu
from jax.sharding import PartitionSpec as P

time_step = 0.3
mass_damping = 0.1
stiff_damping = 0.05
shear_stiff = 0.5
axial_components = (2, 1, 0)
HIGHEST = lax.Precision.HIGHEST
vmem_limit = 48 * 1024 * 1024


def each_other(heights, plan, act):
    h, p = lax.axis_index("height"), lax.axis_index("plan")

    def wrapped(index, size):
        return jnp.where(index >= size, index - size, index)

    def level(up, first):
        above = wrapped(h + up, heights)
        for along in range(first, plan):
            beside = wrapped(p + along, plan)
            act(up * plan + along, above * plan + beside, {"height": above, "plan": beside})

    def turn(up, _):
        level(up, 0)
        return 0

    level(0, 1)
    lax.fori_loop(1, heights, turn, 0)


def signal(semaphore, device):
    pl.semaphore_signal(semaphore, inc=1, device_id=device, device_id_type=pl.DeviceIdType.MESH)


def remote(source, target, send_sem, recv_sem, device):
    return pltpu.make_async_remote_copy(
        src_ref=source,
        dst_ref=target,
        send_sem=send_sem,
        recv_sem=recv_sem,
        device_id=device,
        device_id_type=pl.DeviceIdType.MESH,
    )


def greet_all(heights, plan):
    barrier = pltpu.get_barrier_semaphore()
    each_other(heights, plan, lambda offset, target, device: signal(barrier, device))
    return barrier


def wait_bytes(ref, semaphore):
    pltpu.make_async_copy(ref, ref, semaphore).wait()


def material_props(ids, table_ref):
    kinds = table_ref.shape[0]
    modulus = jnp.full(ids.shape, table_ref[0, 0], jnp.float32)
    yields = jnp.full(ids.shape, 0.4 * table_ref[0, 1], jnp.float32)
    slopes = jnp.full(ids.shape, 0.1 * table_ref[0, 2], jnp.float32)
    for kind in range(1, kinds):
        chosen = ids == kind
        modulus = jnp.where(chosen, table_ref[kind, 0], modulus)
        yields = jnp.where(chosen, 0.4 * table_ref[kind, 1], yields)
        slopes = jnp.where(chosen, 0.1 * table_ref[kind, 2], slopes)
    return modulus, yields, slopes, 1.0 / (modulus + slopes)


def fibre_step(stretch, plastic, harden, modulus, yields, slopes, inverse):
    trial = modulus * (stretch - plastic)
    excess = jnp.abs(trial) - (yields + slopes * harden)
    growth = jnp.maximum(excess, 0.0) * inverse
    signed = jnp.where(trial < 0.0, -growth, growth)
    return trial - modulus * signed, plastic + signed, harden + growth


def steps_kernel(
    heights, plan,
    disp_in, velo_in, mass_in, plastic_in, harden_in, ids_in, table_ref, accel_ref, part_ref,
    disp_out, velo_out, plastic_out, harden_out, snaps_out, gram_ref,
    velos, props, top_plastic, top_harden, top_ids, top_props,
    near_disp, near_velo, edge_send, edge_recv,
    disp_send_sem, disp_recv_sem, velo_send_sem, velo_recv_sem, state_send_sem, state_recv_sem,
    landed, total, part_send_sem, part_recv_sem, give_sem, take_sem,
):
    h, p = lax.axis_index("height"), lax.axis_index("plan")
    fibres = plastic_in.shape[1]
    rows, columns = mass_in.shape
    steps = accel_ref.shape[0]
    has_below, has_above = h > 0, h < heights - 1
    below = {"height": h - 1, "plan": p}
    above = {"height": h + 1, "plan": p}
    left = {"height": h, "plan": lax.rem(p + plan - 1, plan)}
    right = {"height": h, "plan": lax.rem(p + 1, plan)}
    lane = lax.broadcasted_iota(jnp.int32, (rows, columns), 1)
    row = lax.broadcasted_iota(jnp.int32, (rows, columns), 0)
    last = columns - 1

    count = heights * plan
    me = h * plan + p
    barrier = greet_all(heights, plan)

    velos[0] = velo_in[...]
    packed = [jnp.zeros((rows, columns), jnp.float32) for _ in range(3)]
    for f in range(fibres):
        for part, value in enumerate(
            (plastic_in[2, f], harden_in[2, f], ids_in[2, f].astype(jnp.float32))
        ):
            packed[part] = jnp.where(lane == f, value[:, 0:1], packed[part])
    for part in range(3):
        edge_send[part] = packed[part]

    pl.semaphore_wait(barrier, count - 1)

    def disp_copy(side, device):
        return remote(
            disp_in, near_disp.at[side], disp_send_sem.at[side], disp_recv_sem.at[side], device
        )

    def velo_copy(side, step, device):
        return remote(
            velos.at[step], near_velo.at[step, side],
            velo_send_sem.at[step, side], velo_recv_sem.at[step, side], device,
        )

    def state_copies():
        return [
            remote(plastic_in.at[0], top_plastic, state_send_sem.at[0], state_recv_sem.at[0], below),
            remote(harden_in.at[0], top_harden, state_send_sem.at[1], state_recv_sem.at[1], below),
            remote(ids_in.at[0], top_ids, state_send_sem.at[2], state_recv_sem.at[2], below),
        ]

    edge_copy = remote(edge_send, edge_recv, state_send_sem.at[3], state_recv_sem.at[3], left)

    def exchange(step, first):
        copies = [lambda s, d: velo_copy(s, step, d)]
        if first:
            copies.append(disp_copy)

        @pl.when(has_above)
        def _():
            for make in copies:
                make(0, above).start()

        @pl.when(has_below)
        def _():
            for make in copies:
                make(1, below).start()

        for make in copies:
            make(2, right).start()
            make(3, left).start()

    def finish(step, first):
        copies = [lambda s, d: velo_copy(s, step, d)]
        if first:
            copies.append(disp_copy)

        @pl.when(has_below)
        def _():
            for make in copies:
                make(0, below).wait_recv()
                make(1, below).wait_send()

        @pl.when(has_above)
        def _():
            for make in copies:
                make(1, above).wait_recv()
                make(0, above).wait_send()

        for make in copies:
            for side, device in ((2, right), (3, left)):
                make(side, device).wait()

    exchange(0, True)
    edge_copy.start()

    @pl.when(has_below)
    def _():
        for copy in state_copies():
            copy.start()

    def send_part(offset, target, device):
        remote(
            part_ref.at[target], landed.at[offset - 1], part_send_sem, part_recv_sem, device
        ).start()

    each_other(heights, plan, send_part)

    def give_total(offset, target, device):
        remote(total, gram_ref.at[me], give_sem, take_sem, device).start()

    @pl.when(jnp.logical_not(has_below))
    def _():
        near_disp[0] = jnp.zeros(near_disp.shape[1:], jnp.float32)
        for step in range(steps):
            near_velo[step, 0] = jnp.zeros(near_velo.shape[2:], jnp.float32)

    @pl.when(jnp.logical_not(has_above))
    def _():
        near_disp[1] = jnp.zeros(near_disp.shape[1:], jnp.float32)
        for step in range(steps):
            near_velo[step, 1] = jnp.zeros(near_velo.shape[2:], jnp.float32)
        top_plastic[...] = jnp.zeros(top_plastic.shape, jnp.float32)
        top_harden[...] = jnp.zeros(top_harden.shape, jnp.float32)
        top_ids[...] = jnp.zeros(top_ids.shape, jnp.int32)

    zero = jnp.zeros((rows, columns), jnp.float32)

    def own_props(f, sums):
        new_sums = []
        for b in range(3):
            found = material_props(ids_in[b, f], table_ref)
            for part in range(4):
                props[part, b, f] = found[part]
            new_sums.append(sums[b] + found[0])
        return tuple(new_sums)

    sums = lax.fori_loop(0, fibres, own_props, (zero, zero, zero))
    tangents = [total * (1.0 / fibres) for total in sums]

    finish(0, True)
    edge_copy.wait()

    @pl.when(has_below)
    def _():
        for copy in state_copies():
            copy.wait_send()

    @pl.when(has_above)
    def _():
        for copy in state_copies():
            copy.wait_recv()

    def above_props(f, total):
        found = material_props(top_ids[f], table_ref)
        for part in range(4):
            top_props[part, f] = found[part]
        return total + found[0]

    top_tangent = lax.fori_loop(0, fibres, above_props, zero) * (1.0 / fibres)

    in_edge = lane < fibres
    edge_plastic, edge_harden = edge_recv[0], edge_recv[1]
    edge_found = material_props(edge_recv[2].astype(jnp.int32), table_ref)

    def edge_mean(value):
        return jnp.sum(jnp.where(in_edge, value, 0.0), axis=1, keepdims=True) * (1.0 / fibres)

    edge_tangent = edge_mean(edge_found[0])

    disp = [disp_in[c] for c in range(3)]
    velo = [velo_in[c] for c in range(3)]
    mass_inverse = 1.0 / mass_in[...]

    def rows_before(x):
        return jnp.where(row == 0, 0.0, pltpu.roll(x, 1, 0))

    def rows_after(x):
        return jnp.where(row == rows - 1, 0.0, pltpu.roll(x, rows - 1, 0))

    def rim_before(x, left_block):
        return pltpu.roll(jnp.where(lane == last, left_block, x), 1, 1)

    def shear(stretch, rate):
        return shear_stiff * (stretch + stiff_damping * rate)

    for step in range(steps):
        if step > 0:
            finish(step, False)
            for side in range(4):
                for c in range(3):
                    near_disp[side, c] = near_disp[side, c] + time_step * near_velo[step, side, c]
        source_plastic, source_harden = (
            (plastic_in, harden_in) if step == 0 else (plastic_out, harden_out)
        )
        stretch = [
            [disp[c] - near_disp[0, c] for c in range(3)],
            [disp[c] - rows_before(disp[c]) for c in range(3)],
            [disp[c] - rim_before(disp[c], near_disp[2, c]) for c in range(3)],
        ]
        rate = [
            [velo[c] - near_velo[step, 0, c] for c in range(3)],
            [velo[c] - rows_before(velo[c]) for c in range(3)],
            [velo[c] - rim_before(velo[c], near_velo[step, 2, c]) for c in range(3)],
        ]
        top_stretch = [near_disp[1, c] - disp[c] for c in range(3)]
        top_rate = [near_velo[step, 1, c] - velo[c] for c in range(3)]
        rim_stretch = [near_disp[3, c][:, 0:1] - disp[c][:, last:] for c in range(3)]
        rim_rate = [near_velo[step, 3, c][:, 0:1] - velo[c][:, last:] for c in range(3)]

        def fibre(f, totals):
            new_totals = []
            for b in range(3):
                stress, plastic, harden = fibre_step(
                    stretch[b][axial_components[b]], source_plastic[b, f], source_harden[b, f],
                    props[0, b, f], props[1, b, f], props[2, b, f], props[3, b, f],
                )
                plastic_out[b, f] = plastic
                harden_out[b, f] = harden
                new_totals.append(totals[b] + stress)
            stress, plastic, harden = fibre_step(
                top_stretch[axial_components[0]], top_plastic[f], top_harden[f],
                top_props[0, f], top_props[1, f], top_props[2, f], top_props[3, f],
            )
            top_plastic[f] = plastic
            top_harden[f] = harden
            new_totals.append(totals[3] + stress)
            return tuple(new_totals)

        totals = lax.fori_loop(0, fibres, fibre, (zero, zero, zero, zero))
        edge_stress, edge_plastic, edge_harden = fibre_step(
            rim_stretch[axial_components[2]], edge_plastic, edge_harden, *edge_found
        )
        edge_axial = edge_mean(edge_stress)

        new_velo = []
        for c in range(3):
            force = []
            for b in range(3):
                if c == axial_components[b]:
                    force.append(
                        totals[b] * (1.0 / fibres) + stiff_damping * tangents[b] * rate[b][c]
                    )
                else:
                    force.append(shear(stretch[b][c], rate[b][c]))
            if c == axial_components[0]:
                top = totals[3] * (1.0 / fibres) + stiff_damping * top_tangent * top_rate[c]
            else:
                top = shear(top_stretch[c], top_rate[c])
            if c == axial_components[2]:
                rim = edge_axial + stiff_damping * edge_tangent * rim_rate[c]
            else:
                rim = shear(rim_stretch[c], rim_rate[c])
            top = jnp.where(has_above, top, 0.0)
            after_rim = jnp.where(lane == last, rim, pltpu.roll(force[2], last, 1))
            resisting = (
                force[0] - top + (force[1] - rows_after(force[1])) + (force[2] - after_rim)
            )
            acceleration = -accel_ref[step, c] - resisting * mass_inverse
            new_velo.append(
                ((1.0 - 0.5 * mass_damping * time_step) * velo[c] + time_step * acceleration)
                * (1.0 / (1.0 + 0.5 * mass_damping * time_step))
            )
        velo = new_velo
        if step + 1 < steps:
            for c in range(3):
                velos[step + 1, c] = velo[c]
            exchange(step + 1, False)
        if step == 0:
            wait_bytes(landed, part_recv_sem)
            total[...] = part_ref[me] + jnp.sum(landed[...], axis=0)
            each_other(heights, plan, give_total)
            gram_ref[me] = total[...]
        for c in range(3):
            disp[c] = disp[c] + time_step * velo[c]
            snaps_out[step, c] = disp[c].astype(jnp.bfloat16)
    for c in range(3):
        disp_out[c] = disp[c]
        velo_out[c] = velo[c]
    wait_bytes(landed, take_sem)
    wait_bytes(landed, part_send_sem)
    wait_bytes(landed, give_sem)


def run_steps(disp, velo, mass, plastic, harden, ids, table, accel, part):
    heights, plan = lax.axis_size("height"), lax.axis_size("plan")
    steps = accel.shape[0]
    vmem = pl.BlockSpec(memory_space=pltpu.VMEM)
    smem = pl.BlockSpec(memory_space=pltpu.SMEM)
    f32 = jnp.float32
    fibres = plastic.shape[1]
    plane = mass.shape
    count = heights * plan
    modes = part.shape[0]
    blocks = (count, modes // count, modes)
    *ends, gram = pl.pallas_call(
        functools.partial(steps_kernel, heights, plan),
        out_shape=(
            jax.ShapeDtypeStruct(disp.shape, f32),
            jax.ShapeDtypeStruct(velo.shape, f32),
            jax.ShapeDtypeStruct(plastic.shape, f32),
            jax.ShapeDtypeStruct(harden.shape, f32),
            jax.ShapeDtypeStruct((steps,) + disp.shape, jnp.bfloat16),
            jax.ShapeDtypeStruct(blocks, f32),
        ),
        in_specs=[vmem] * 6 + [smem] * 2 + [vmem],
        out_specs=(vmem,) * 6,
        scratch_shapes=[
            pltpu.VMEM((steps,) + velo.shape, f32),
            pltpu.VMEM((4,) + plastic.shape, f32),
            pltpu.VMEM((fibres,) + plane, f32),
            pltpu.VMEM((fibres,) + plane, f32),
            pltpu.VMEM((fibres,) + plane, jnp.int32),
            pltpu.VMEM((4, fibres) + plane, f32),
            pltpu.VMEM((4,) + disp.shape, f32),
            pltpu.VMEM((steps, 4) + velo.shape, f32),
            pltpu.VMEM((3,) + plane, f32),
            pltpu.VMEM((3,) + plane, f32),
            pltpu.SemaphoreType.DMA((4,)),
            pltpu.SemaphoreType.DMA((4,)),
            pltpu.SemaphoreType.DMA((steps, 4)),
            pltpu.SemaphoreType.DMA((steps, 4)),
            pltpu.SemaphoreType.DMA((4,)),
            pltpu.SemaphoreType.DMA((4,)),
            pltpu.VMEM((count - 1,) + blocks[1:], f32),
            pltpu.VMEM(blocks[1:], f32),
        ]
        + [pltpu.SemaphoreType.DMA] * 4,
        compiler_params=pltpu.CompilerParams(
            collective_id=0, has_side_effects=True, vmem_limit_bytes=vmem_limit
        ),
        name="time_steps",
    )(disp, velo, mass, plastic, harden, ids, table, accel, part.reshape(blocks))
    return *ends, gram.reshape(modes, modes)


def coords_kernel(heights, plan, part_ref, out_ref, landed, send_sem, recv_sem):
    count = heights * plan
    me = lax.axis_index("height") * plan + lax.axis_index("plan")
    barrier = greet_all(heights, plan)
    pl.semaphore_wait(barrier, count - 1)

    def send(offset, target, device):
        remote(
            part_ref.at[target], landed.at[offset - 1], send_sem, recv_sem, device
        ).start()

    each_other(heights, plan, send)
    wait_bytes(landed, recv_sem)
    out_ref[...] = part_ref[me] + jnp.sum(landed[...], axis=0)
    wait_bytes(landed, send_sem)


def coords_total(part):
    plan = lax.axis_size("plan")
    count = lax.axis_size(("height", "plan"))
    modes, snaps = part.shape
    rows = modes // count
    vmem = pl.BlockSpec(memory_space=pltpu.VMEM)
    return pl.pallas_call(
        functools.partial(coords_kernel, lax.axis_size("height"), plan),
        out_shape=jax.ShapeDtypeStruct((rows, snaps), jnp.float32),
        in_specs=[vmem],
        out_specs=vmem,
        scratch_shapes=[pltpu.VMEM((count - 1, rows, snaps), jnp.float32)]
        + [pltpu.SemaphoreType.DMA] * 2,
        compiler_params=pltpu.CompilerParams(
            collective_id=2, has_side_effects=True, vmem_limit_bytes=vmem_limit
        ),
        name="coords_sum",
    )(part.reshape(count, rows, snaps))


def solve_kernel(gram_ref, projected_ref, *refs):
    kept = (len(refs) - 2) // 2
    held, out_ref, handed, sems = refs[:kept], refs[kept], refs[kept + 1 : -1], refs[-1]
    copies = [
        pltpu.make_async_copy(source, target, sems.at[i])
        for i, (source, target) in enumerate(zip(held, handed))
    ]
    for copy in copies:
        copy.start()
    modes = gram_ref.shape[0]
    row = lax.broadcasted_iota(jnp.int32, (modes, modes), 0)
    column = lax.broadcasted_iota(jnp.int32, (modes, modes), 1)
    lower = jnp.where(row >= column, gram_ref[...], 0.0)
    gram = lower + jnp.where(row == column, 0.0, lower).T
    identity = jnp.where(row == column, 1.0, 0.0)
    size = jnp.max(jnp.sum(jnp.abs(gram), axis=0))
    guess = identity * (1.0 / size)
    rough_gram = gram.astype(jnp.bfloat16)

    def multiply(a, b):
        return jnp.dot(a, b, precision=HIGHEST, preferred_element_type=jnp.float32)

    def rough_multiply(a, b):
        return jnp.dot(a, b, preferred_element_type=jnp.float32)

    def length(residual):
        return jnp.max(jnp.sum(jnp.abs(residual), axis=0))

    def rough_unfinished(state):
        turns, error, _ = state
        return jnp.logical_and(turns < 12, error > 0.1)

    def rough_improve(state):
        turns, _, inverse = state
        narrow = inverse.astype(jnp.bfloat16)
        residual = identity - rough_multiply(rough_gram, narrow)
        step = rough_multiply(narrow, residual.astype(jnp.bfloat16))
        return turns + 1, length(residual), inverse + step

    _, _, start = lax.while_loop(rough_unfinished, rough_improve, (0, jnp.float32(2.0), guess))
    residual = identity - multiply(gram, start)
    usable = length(residual) < 0.9
    start = jnp.where(usable, start, guess)
    residual = jnp.where(usable, residual, identity - gram * (1.0 / size))

    def unfinished(state):
        turns, error, _, _ = state
        return jnp.logical_and(turns < 60, error > 3e-3)

    def improve(state):
        turns, _, inverse, residual = state
        inverse = inverse + multiply(inverse, residual)
        residual = identity - multiply(gram, inverse)
        return turns + 1, length(residual), inverse, residual

    _, _, inverse, residual = lax.while_loop(
        unfinished, improve, (0, length(residual), start, residual)
    )
    projected = projected_ref[...]
    out_ref[...] = multiply(inverse, projected + multiply(residual, projected))
    for copy in copies:
        copy.wait()


def solve(gram, projected, held):
    vmem = pl.BlockSpec(memory_space=pltpu.VMEM)
    anywhere = pl.BlockSpec(memory_space=pl.ANY)
    return pl.pallas_call(
        solve_kernel,
        out_shape=(jax.ShapeDtypeStruct(projected.shape, jnp.float32),)
        + tuple(jax.ShapeDtypeStruct(x.shape, x.dtype) for x in held),
        in_specs=[vmem, vmem] + [anywhere] * len(held),
        out_specs=(vmem,) + (anywhere,) * len(held),
        scratch_shapes=[pltpu.SemaphoreType.DMA((len(held),))],
        compiler_params=pltpu.CompilerParams(vmem_limit_bytes=vmem_limit),
        name="solve",
    )(gram, projected, *held)


def products_kernel(
    modes_ref, mass_ref, history_ref, gram_ref, projected_ref, weighted_ref, modes_wide, snaps_wide
):
    modes, rows, columns = modes_ref.shape
    earlier, snaps = history_ref.shape[0], projected_ref.shape[1]
    chunk = math.gcd(modes, 16)
    group = math.gcd(rows, 8)

    def widen(i, _):
        block = modes_ref[pl.ds(i * chunk, chunk)].astype(jnp.float32)
        modes_wide[pl.ds(pl.multiple_of(i * chunk * rows, 8), chunk * rows), :] = block.reshape(
            chunk * rows, columns
        )
        return 0

    lax.fori_loop(0, modes // chunk, widen, 0)

    def widen_history(i, _):
        snaps_wide[pl.ds(pl.multiple_of(i * rows, 8), rows), :] = history_ref[i].astype(jnp.float32)
        return 0

    lax.fori_loop(0, earlier, widen_history, 0)
    snaps_wide[earlier * rows :, :] = jnp.zeros(((snaps - earlier) * rows, columns), jnp.float32)

    @pl.when(pl.program_id(0) == 0)
    def _():
        gram_ref[...] = jnp.zeros(gram_ref.shape, jnp.float32)
        projected_ref[...] = jnp.zeros(projected_ref.shape, jnp.float32)

    contract_last = (((1,), (1,)), ((), ()))

    def add(i, _):
        weighted, plain, shots = [], [], []
        masses = mass_ref[pl.ds(pl.multiple_of(i * group, group), group), :]
        for j in range(group):
            row = i * group + j
            shape = modes_wide[pl.ds(row, modes, stride=rows), :]
            weighted.append((shape * masses[j : j + 1, :]).astype(jnp.bfloat16))
            plain.append(shape.astype(jnp.bfloat16))
            shots.append(snaps_wide[pl.ds(row, snaps, stride=rows), :].astype(jnp.bfloat16))
        left = jnp.concatenate(weighted, axis=1)
        weighted_ref[i] = left
        gram_ref[...] += lax.dot_general(
            left, jnp.concatenate(plain, axis=1), contract_last,
            preferred_element_type=jnp.float32,
        )
        projected_ref[...] += lax.dot_general(
            left, jnp.concatenate(shots, axis=1), contract_last,
            preferred_element_type=jnp.float32,
        )
        return 0

    lax.fori_loop(0, rows // group, add, 0)


def products(mode_shapes, mass, history, snaps):
    modes, parts, rows, columns = mode_shapes.shape
    earlier = history.shape[0]
    group = math.gcd(rows, 8)
    wide = (rows // group, modes, group * columns)
    f32 = jnp.float32
    return pl.pallas_call(
        products_kernel,
        grid=(parts,),
        out_shape=(
            jax.ShapeDtypeStruct((modes, modes), f32),
            jax.ShapeDtypeStruct((modes, snaps), f32),
            jax.ShapeDtypeStruct((parts,) + wide, jnp.bfloat16),
        ),
        in_specs=[
            pl.BlockSpec((modes, None, rows, columns), lambda c: (0, c, 0, 0)),
            pl.BlockSpec((rows, columns), lambda c: (0, 0)),
            pl.BlockSpec((earlier, None, rows, columns), lambda c: (0, c, 0, 0)),
        ],
        out_specs=(
            pl.BlockSpec((modes, modes), lambda c: (0, 0)),
            pl.BlockSpec((modes, snaps), lambda c: (0, 0)),
            pl.BlockSpec((None,) + wide, lambda c: (c, 0, 0, 0)),
        ),
        scratch_shapes=[
            pltpu.VMEM((modes * rows, columns), f32),
            pltpu.VMEM((snaps * rows, columns), f32),
        ],
        compiler_params=pltpu.CompilerParams(vmem_limit_bytes=vmem_limit),
        name="products",
    )(mode_shapes, mass, history)


def recent_kernel(weighted_ref, recent_ref, before_ref, projected_ref, snaps_wide):
    groups, modes, depth = weighted_ref.shape
    recent, rows, columns = recent_ref.shape
    snaps = projected_ref.shape[1]
    earlier = snaps - recent
    group = rows // groups

    @pl.when(pl.program_id(0) == 0)
    def _():
        snaps_wide[: earlier * rows, :] = jnp.zeros((earlier * rows, columns), jnp.float32)
        projected_ref[...] = before_ref[...]

    for i in range(recent):
        snaps_wide[pl.ds((earlier + i) * rows, rows), :] = recent_ref[i].astype(jnp.float32)
    for i in range(groups):
        shots = [
            snaps_wide[pl.ds(i * group + j, snaps, stride=rows), :].astype(jnp.bfloat16)
            for j in range(group)
        ]
        projected_ref[...] += lax.dot_general(
            weighted_ref[i], jnp.concatenate(shots, axis=1), (((1,), (1,)), ((), ())),
            preferred_element_type=jnp.float32,
        )


def add_recent(weighted, recent, before):
    parts, groups, modes, depth = weighted.shape
    later, _, rows, columns = recent.shape
    snaps = before.shape[1]
    return pl.pallas_call(
        recent_kernel,
        grid=(parts,),
        out_shape=jax.ShapeDtypeStruct(before.shape, jnp.float32),
        in_specs=[
            pl.BlockSpec((None, groups, modes, depth), lambda c: (c, 0, 0, 0)),
            pl.BlockSpec((later, None, rows, columns), lambda c: (0, c, 0, 0)),
            pl.BlockSpec((modes, snaps), lambda c: (0, 0)),
        ],
        out_specs=pl.BlockSpec((modes, snaps), lambda c: (0, 0)),
        scratch_shapes=[pltpu.VMEM((snaps * rows, columns), jnp.float32)],
        compiler_params=pltpu.CompilerParams(vmem_limit_bytes=vmem_limit),
        name="recent_products",
    )(weighted, recent, before)


def body(
    displacement,
    velocity,
    lumped_mass,
    plastic_strain,
    hardening_strain,
    material_ids,
    material_table,
    ground_accel,
    snapshot_history,
    mode_shapes,
):
    snaps = snapshot_history.shape[0] + ground_accel.shape[0]
    mass_gram, projected, weighted = products(
        mode_shapes[:, :, 0], lumped_mass[0], snapshot_history[:, :, 0], snaps
    )
    disp_end, velo_end, plastic_end, harden_end, new_snaps, gram = run_steps(
        displacement[:, 0], velocity[:, 0], lumped_mass[0], plastic_strain[:, :, 0],
        hardening_strain[:, :, 0], material_ids[:, :, 0], material_table, ground_accel, mass_gram,
    )
    projected = add_recent(weighted, new_snaps, projected)
    coords, disp_end, velo_end, plastic_end, harden_end = solve(
        gram, projected, (disp_end, velo_end, plastic_end, harden_end)
    )
    modal_coords = coords_total(coords)
    return (
        disp_end[:, None], velo_end[:, None], plastic_end[:, :, None], harden_end[:, :, None],
        modal_coords,
    )


def solution(mesh):
    return jax.shard_map(
        body,
        mesh=mesh,
        in_specs=(
            P(None, "height", None, "plan"),
            P(None, "height", None, "plan"),
            P("height", None, "plan"),
            P(None, None, "height", None, "plan"),
            P(None, None, "height", None, "plan"),
            P(None, None, "height", None, "plan"),
            P(),
            P(),
            P(None, None, "height", None, "plan"),
            P(None, None, "height", None, "plan"),
        ),
        out_specs=(
            P(None, "height", None, "plan"),
            P(None, "height", None, "plan"),
            P(None, None, "height", None, "plan"),
            P(None, None, "height", None, "plan"),
            P(("height", "plan"), None),
        ),
        check_vma=False,
    )
```
